256 devices in a mesh: dp: 16 (over y_lo, x, core), ctx: 16 (over y_hi, z).
Axes of the slice: x: 4, y: 4 (y_hi: 2, y_lo: 2; y = y_hi * 2 + y_lo), z: 8, core: 2. Of those that a mesh axis runs over, the one named last changes fastest.
Arguments:
- query: bfloat16 [16, 2048, 1024], P('dp', 'ctx'), may hold values from -5 to 5
- key: bfloat16 [16, 2048, 128], P('dp', 'ctx'), may hold values from -5 to 5
- value: bfloat16 [16, 2048, 128], P('dp', 'ctx'), may hold values from -6 to 6
- output: bfloat16 [16, 2048, 1024], P('dp', 'ctx'), may hold values from -6 to 6
- output_cotangent: bfloat16 [16, 2048, 1024], P('dp', 'ctx'), may hold values from -6 to 6
- inputs: bfloat16 [32768, 8192], P(('dp', 'ctx')), may hold values from -0.125 to 0.125
- doc_lengths: int32 [16, 8], P('dp'), may hold values from 1 to 1024, 2048 in all within a row
- block_order: int32 [32], replicated, may hold values from 0 to 31, each once
Outputs:
- d_query: bfloat16 [16, 2048, 1024], P('dp', 'ctx')
- d_key: bfloat16 [16, 2048, 128], P('dp', 'ctx')
- value_gradient: bfloat16 [16, 2048, 128], P('dp', 'ctx')
- value_weight_gradient: float32 [8192, 128], P(('dp', 'ctx'))
The draws below stay inside these ranges and needn't reach their ends.
Inputs may be any that keep to these rules, and one draw needn't show every extreme that they name: `doc_lengths`: row s lists in order the lengths of the 8 documents packed into sequence s; they add up to 2048 and the longest has exactly 1024 tokens. Storage block c of every sequence (storage rows c * 64 onward) holds the sequence's block block_order[c] of 64 tokens; each number appears once.
All inputs are finite; a program needn't handle non-finite values.
Results may differ from the reference program's by a relative error of at most 0.015.
Values may be sent and summed in bfloat16 or wider, within the bound.
No kernel may reach another device: no remote copies, remote signals or barrier semaphores. Data moves between devices by JAX's collectives and lax.ppermute only.
A program may use at most 64 MiB of HBM per device.

```python
import math
import jax
import jax.numpy as jnp
import numpy as np
from jax import lax

D = 8192
HEAD_SIZE = 128
KEY_VALUE_HEADS = 1
QUERY_HEADS = 8
ROWS = 128
NDOC = 8
SEQUENCE_COUNT = 16
SEQUENCE_LENGTH = 2048
TOKEN_COUNT = 32768
BLOCKS = 32
BLOCK = 64
MOST = 1024
N_CTX = 16


def draw_query(key, part):
    key = jax.random.fold_in(key, 1)
    sampled_arrays = jnp.clip(jax.random.normal(key, (SEQUENCE_COUNT, SEQUENCE_LENGTH, KEY_VALUE_HEADS, QUERY_HEADS // KEY_VALUE_HEADS, HEAD_SIZE), jnp.float32), -5.0, 5.0)
    return sampled_arrays.reshape(SEQUENCE_COUNT, SEQUENCE_LENGTH, QUERY_HEADS * HEAD_SIZE).astype(jnp.bfloat16)


def draw_key(key, part):
    key = jax.random.fold_in(key, 2)
    sampled_arrays = jnp.clip(jax.random.normal(key, (SEQUENCE_COUNT, SEQUENCE_LENGTH, KEY_VALUE_HEADS, HEAD_SIZE), jnp.float32), -5.0, 5.0)
    return sampled_arrays.reshape(SEQUENCE_COUNT, SEQUENCE_LENGTH, KEY_VALUE_HEADS * HEAD_SIZE).astype(jnp.bfloat16)


def strengthened(entries, rng, source, target, shards_of, factor):
    owner, partner = [(jnp.arange(entries.shape[dim]) // (entries.shape[dim] // shards_of)).reshape([-1 if axis == dim else 1 for axis in range(entries.ndim)]) for dim in (source, target)]
    chosen = jax.random.permutation(rng, shards_of)[partner]
    strong = (owner == chosen) | (owner == (partner + shards_of // 2) % shards_of)
    return jnp.where(strong, factor * entries, entries)


def block_scale(rng, shape, cuts, least, top_value):
    level, own = 1.0, jax.random.fold_in(rng, 6)
    for dim, shards_of in cuts:
        steps = jnp.exp(jax.random.uniform(jax.random.fold_in(own, dim), (shards_of,), jnp.float32, least / len(cuts), top_value / len(cuts)))
        level = level * jnp.repeat(steps, shape[dim] // shards_of).reshape([-1 if axis == dim else 1 for axis in range(len(shape))])
    return level


def length_profile(count, total, most, slope):
    weights = [(1 << 20) // math.isqrt(grade ** slope) + 1 for grade in range(2, count + 1)]
    surplus, counts = total - most - (count - 1), [1] * (count - 1)
    while surplus > 0:
        candidates = [i for i in range(count - 1) if counts[i] < most]
        mass, remaining = sum([weights[i] for i in candidates]), surplus
        for i in candidates:
            more = min(most - counts[i], max(1, remaining * weights[i] // mass), surplus)
            counts[i] = counts[i] + more
            surplus = surplus - more
    return np.array([most] + counts)


def uneven_parts(own_key, number_of, total, reach, lean):
    if number_of == 2:
        one = jax.random.randint(own_key, (), max(1, total - reach), min(reach, total - 1) + 1)
        return jnp.stack([one, total - one])
    tallies = jnp.asarray(length_profile(number_of, total, reach, lean), jnp.int32)
    couples = (number_of - 1) // 2
    source_of, taker = tallies[1:1 + 2 * couples:2], tallies[2:2 + 2 * couples:2]
    slack = jnp.minimum(source_of - 1, reach - taker)
    moved = jax.random.randint(jax.random.fold_in(own_key, 1), (couples,), 0, 1 << 20) % (slack + 1)
    tallies = tallies.at[1:1 + 2 * couples:2].set(source_of - moved).at[2:2 + 2 * couples:2].set(taker + moved)
    return tallies[jax.random.permutation(jax.random.fold_in(own_key, 2), number_of)]


def normal_values(own_key, extent, width, most, cuts=(), kind=jnp.bfloat16):
    drawn = width * jax.random.normal(own_key, extent, jnp.float32)
    if cuts:
        drawn = drawn * block_scale(own_key, extent, cuts, -0.22, 0.18)
    return jnp.clip(drawn, -most, most).astype(kind)


def heavy_noise(stream_key, dims, deviation, limit, pieces, heavy, kind=jnp.bfloat16):
    values = deviation * jax.random.normal(stream_key, dims, jnp.float32)
    if pieces:
        values = values * block_scale(stream_key, dims, pieces, -0.22, 0.18)
    return jnp.clip(strengthened(values, jax.random.fold_in(stream_key, 3), *heavy), -limit, limit).astype(kind)


def setup_inputs(seed: int = 0) -> dict:
    arg_keys = jax.random.split(jax.random.key(seed), 9)
    query = draw_query(jax.random.fold_in(arg_keys[8], 71), 0)
    key = draw_key(jax.random.fold_in(arg_keys[8], 71), 0)
    value = normal_values(arg_keys[2], (SEQUENCE_COUNT, SEQUENCE_LENGTH, KEY_VALUE_HEADS * HEAD_SIZE), 1.0, 6.0, ((0, 16), (1, 16)))
    output = normal_values(arg_keys[3], (SEQUENCE_COUNT, SEQUENCE_LENGTH, QUERY_HEADS * HEAD_SIZE), 1.0, 6.0, ((0, 16), (1, 16)))
    output_cotangent = normal_values(arg_keys[4], (SEQUENCE_COUNT, SEQUENCE_LENGTH, QUERY_HEADS * HEAD_SIZE), 1.0, 6.0, ((0, 16), (1, 16)))
    inputs = heavy_noise(arg_keys[5], (TOKEN_COUNT, D), (TOKEN_COUNT ** -0.5), 0.125, ((0, 256),), (0, 1, 256, 6.0))
    doc_lengths = jax.vmap(lambda own: uneven_parts(own, NDOC, SEQUENCE_LENGTH, MOST, 2))(jax.random.split(arg_keys[6], SEQUENCE_COUNT)).reshape((SEQUENCE_COUNT, NDOC)).astype(jnp.int32)
    block_order = jax.random.permutation(arg_keys[7], BLOCKS).astype(jnp.int32)
    return dict(query=query, key=key, value=value, output=output, output_cotangent=output_cotangent, inputs=inputs, doc_lengths=doc_lengths, block_order=block_order)


score_with_mask = -1e30


def reference(query, key, value, output, output_cotangent, inputs, doc_lengths, block_order):
    query_group_width = QUERY_HEADS // KEY_VALUE_HEADS
    score_scale = HEAD_SIZE ** -0.5
    storage = jnp.arange(SEQUENCE_LENGTH, dtype=jnp.int32)
    position = block_order[storage // BLOCK] * BLOCK + storage % BLOCK

    def sequence(items):
        query_by_sequence, key_by_sequence, value_by_sequence, output_by_sequence, gradient_by_sequence, lengths = items
        doc_ends = jnp.cumsum(lengths)
        segment = jnp.sum((position[:, None] >= doc_ends[None, :]).astype(jnp.int32), axis=1)
        allowed = (segment[:, None] == segment[None, :]) & (position[None, :] <= position[:, None])
        query_by_head = query_by_sequence.reshape(SEQUENCE_LENGTH, KEY_VALUE_HEADS, query_group_width, HEAD_SIZE).transpose(1, 2, 0, 3)
        output_by_head = output_by_sequence.reshape(SEQUENCE_LENGTH, KEY_VALUE_HEADS, query_group_width, HEAD_SIZE).transpose(1, 2, 0, 3)
        gradient_by_head = gradient_by_sequence.reshape(SEQUENCE_LENGTH, KEY_VALUE_HEADS, query_group_width, HEAD_SIZE).transpose(1, 2, 0, 3)
        key_by_head = key_by_sequence.reshape(SEQUENCE_LENGTH, KEY_VALUE_HEADS, HEAD_SIZE).transpose(1, 0, 2)
        value_by_head = value_by_sequence.reshape(SEQUENCE_LENGTH, KEY_VALUE_HEADS, HEAD_SIZE).transpose(1, 0, 2)

        def one_head(parts):
            head_query, head_key, head_value, head_output, head_grad = parts
            key_full = head_key.astype(jnp.float32)
            value_full = head_value.astype(jnp.float32)

            def one_query(qparts):
                single_query, single_output, single_grad = qparts
                query_full = single_query.astype(jnp.float32)
                grad_full = single_grad.astype(jnp.float32)
                scores = jnp.einsum("qd,kd->qk", query_full, key_full) * score_scale
                scores = jnp.where(allowed, scores, score_with_mask)
                top_score = jnp.max(scores, axis=1, keepdims=True)
                lse = top_score + jnp.log(jnp.sum(jnp.exp(scores - top_score), axis=1, keepdims=True))
                probs = jnp.where(allowed, jnp.exp(scores - lse), 0.0)
                probs_low = probs.astype(jnp.bfloat16)
                delta = jnp.sum(grad_full * single_output.astype(jnp.float32), axis=1)[:, None]
                dprobs = jnp.einsum("qd,kd->qk", grad_full, value_full)
                dscores = (probs * (dprobs - delta)).astype(jnp.bfloat16)
                grad_query = (jnp.einsum("qk,kd->qd", dscores.astype(jnp.float32), key_full) * score_scale).astype(jnp.bfloat16)
                score_blocks = dscores.astype(jnp.float32).reshape(N_CTX, ROWS, SEQUENCE_LENGTH)
                prob_blocks = probs_low.astype(jnp.float32).reshape(N_CTX, ROWS, SEQUENCE_LENGTH)
                key_term = jnp.einsum("rqk,rqd->rkd", score_blocks, query_full.reshape(N_CTX, ROWS, HEAD_SIZE))
                value_term = jnp.einsum("rqk,rqd->rkd", prob_blocks, grad_full.reshape(N_CTX, ROWS, HEAD_SIZE))
                return grad_query, key_term, value_term

            grad_query, key_terms, value_terms = lax.map(one_query, (head_query, head_output, head_grad))
            key_part = (jnp.sum(key_terms, axis=0) * score_scale).astype(jnp.bfloat16)
            value_part = jnp.sum(value_terms, axis=0).astype(jnp.bfloat16)
            key_gradient_rows = jnp.sum(key_part.astype(jnp.float32), axis=0).astype(jnp.bfloat16)
            value_gradient_rows = jnp.sum(value_part.astype(jnp.float32), axis=0).astype(jnp.bfloat16)
            return grad_query, key_gradient_rows, value_gradient_rows

        grad_query, key_gradient_rows, value_gradient_rows = lax.map(one_head, (query_by_head, key_by_head, value_by_head, output_by_head, gradient_by_head))
        grad_query = grad_query.transpose(2, 0, 1, 3).reshape(SEQUENCE_LENGTH, QUERY_HEADS * HEAD_SIZE)
        key_gradient_rows = key_gradient_rows.transpose(1, 0, 2).reshape(SEQUENCE_LENGTH, KEY_VALUE_HEADS * HEAD_SIZE)
        value_gradient_rows = value_gradient_rows.transpose(1, 0, 2).reshape(SEQUENCE_LENGTH, KEY_VALUE_HEADS * HEAD_SIZE)
        return grad_query, key_gradient_rows, value_gradient_rows

    d_query, d_key, value_gradient = lax.map(sequence, (query, key, value, output, output_cotangent, doc_lengths))
    value_weight_gradient = jnp.dot(inputs.T, value_gradient.reshape(TOKEN_COUNT, KEY_VALUE_HEADS * HEAD_SIZE), preferred_element_type=jnp.float32)
    return d_query, d_key, value_gradient, value_weight_gradient
```

```python
import functools
import math

import jax
import jax.numpy as jnp
from jax import lax
from jax.experimental import pallas as pl
from jax.experimental.pallas import tpu as pltpu
from jax.sharding import Mesh, PartitionSpec as P

HEAD_SIZE = 128
QUERY_HEADS = 8
BLOCK = 64
BLOCKS = 32
NDOC = 8
ROWS = 128
KEYS = 2048
N_CTX = 16
CHUNK = 256
PAIR = 2 * HEAD_SIZE
PAIRS = QUERY_HEADS // 2
SCALE = HEAD_SIZE**-0.5
SCALE_LOG2 = SCALE * math.log2(math.e)
MASKED = -1e30
VMEM_LIMIT = 48 * 1024 * 1024
NT = (((1,), (1,)), ((), ()))

CTX = ("yhi", "z")
NEAR = ("x", "core")
FAR = ("ylo", "yhi", "z")


def two_heads(block):
    return jnp.concatenate([block[:, :HEAD_SIZE], block[:, HEAD_SIZE:]], axis=0)


def fold_rows(tile, op):
    return op(tile.reshape(tile.shape[0] // 8, 8, tile.shape[1]), axis=0)


def write_bias(scalars, bias):
    lane = lax.broadcasted_iota(jnp.int32, (1, ROWS), 1)
    me = scalars[BLOCKS + NDOC]
    first, second = scalars[2 * me] * BLOCK, scalars[2 * me + 1] * BLOCK
    high = jnp.where(lane < BLOCK, first + lane, second + lane - BLOCK)
    low = jnp.zeros_like(high)
    end = scalars[BLOCKS]
    for doc in range(1, NDOC):
        low = jnp.where(high >= end, end, low)
        end = end + scalars[BLOCKS + doc]
    low = jnp.where(high >= end, end, low)
    row = lax.broadcasted_iota(jnp.int32, (BLOCK, ROWS), 0)

    def one_block(block, carry):
        position = scalars[block] * BLOCK + row
        allowed = (position <= high) & (position >= low)
        start = pl.multiple_of(block * BLOCK, BLOCK)
        bias[pl.ds(start, BLOCK), :] = jnp.where(allowed, 0.0, MASKED)
        return carry

    lax.fori_loop(0, BLOCKS, one_block, 0)


def probs_kernel(scalars, query, cotangent, kv, probs, value_part, bias, scores, value_acc):
    step = pl.program_id(0)

    @pl.when(step == 0)
    def _():
        write_bias(scalars, bias)
        value_acc[...] = jnp.zeros_like(value_acc)

    queries = two_heads(query[...])
    gradients = two_heads(cotangent[...])

    def rows_of(chunk):
        return pl.ds(pl.multiple_of(chunk * CHUNK, CHUNK), CHUNK)

    def score(chunk, top):
        rows = rows_of(chunk)
        raw = lax.dot_general(
            kv[rows, :HEAD_SIZE], queries, NT, preferred_element_type=jnp.float32
        )
        add = bias[rows, :]
        tile = raw * SCALE_LOG2 + jnp.concatenate([add, add], axis=1)
        scores[rows, :] = tile
        return jnp.maximum(top, fold_rows(tile, jnp.max))

    top = lax.fori_loop(0, KEYS // CHUNK, score, jnp.full((8, PAIR), MASKED, jnp.float32))
    top = jnp.max(top, axis=0, keepdims=True)

    def weigh(chunk, total):
        rows = rows_of(chunk)
        tile = jnp.exp2(scores[rows, :] - top)
        scores[rows, :] = tile
        return total + fold_rows(tile, jnp.sum)

    total = lax.fori_loop(0, KEYS // CHUNK, weigh, jnp.zeros((8, PAIR), jnp.float32))
    share = 1.0 / jnp.sum(total, axis=0, keepdims=True)

    def finish(chunk, carry):
        rows = rows_of(chunk)
        low = (scores[rows, :] * share).astype(jnp.bfloat16)
        probs[rows, :] = low
        value_acc[rows, :] += jnp.dot(low, gradients, preferred_element_type=jnp.float32)
        return carry

    lax.fori_loop(0, KEYS // CHUNK, finish, 0)

    @pl.when(step == PAIRS - 1)
    def _():
        value_part[...] = value_acc[...].astype(jnp.bfloat16)


def grads_kernel(
    query, output, cotangent, kv, probs, query_grad, key_part, key_turned, key_acc, query_acc
):
    step = pl.program_id(0)

    @pl.when(step == 0)
    def _():
        key_turned[...] = kv[:, :HEAD_SIZE].T
        key_acc[...] = jnp.zeros_like(key_acc)

    queries = two_heads(query[...])
    gradients = two_heads(cotangent[...])
    product = gradients.astype(jnp.float32) * two_heads(output[...]).astype(jnp.float32)
    delta = jnp.concatenate(
        [
            jnp.sum(product[:ROWS].T, axis=0, keepdims=True),
            jnp.sum(product[ROWS:].T, axis=0, keepdims=True),
        ],
        axis=1,
    )
    query_acc[...] = jnp.zeros_like(query_acc)
    for chunk in range(KEYS // CHUNK):
        rows = pl.ds(chunk * CHUNK, CHUNK)
        dprobs = lax.dot_general(
            kv[rows, HEAD_SIZE:], gradients, NT, preferred_element_type=jnp.float32
        )
        dscores = (probs[rows, :].astype(jnp.float32) * (dprobs - delta)).astype(jnp.bfloat16)
        key_acc[rows, :] += jnp.dot(dscores, queries, preferred_element_type=jnp.float32)
        query_acc[...] += jnp.dot(
            key_turned[:, rows], dscores, preferred_element_type=jnp.float32
        )
    turned = query_acc[...] * SCALE
    query_grad[:, :HEAD_SIZE] = turned[:, :ROWS].T.astype(jnp.bfloat16)
    query_grad[:, HEAD_SIZE:] = turned[:, ROWS:].T.astype(jnp.bfloat16)

    @pl.when(step == PAIRS - 1)
    def _():
        key_part[...] = (key_acc[...] * SCALE).astype(jnp.bfloat16)


def pair_block(step):
    return (0, step)


def whole(step):
    return (0, 0)


def attention_probs(scalars, query, cotangent, kv):
    return pl.pallas_call(
        probs_kernel,
        grid=(PAIRS,),
        in_specs=[
            pl.BlockSpec(memory_space=pltpu.SMEM),
            pl.BlockSpec((ROWS, PAIR), pair_block),
            pl.BlockSpec((ROWS, PAIR), pair_block),
            pl.BlockSpec((KEYS, 2 * HEAD_SIZE), whole),
        ],
        out_specs=[
            pl.BlockSpec((KEYS, PAIR), pair_block),
            pl.BlockSpec((KEYS, HEAD_SIZE), whole),
        ],
        out_shape=[
            jax.ShapeDtypeStruct((KEYS, QUERY_HEADS * ROWS), jnp.bfloat16),
            jax.ShapeDtypeStruct((KEYS, HEAD_SIZE), jnp.bfloat16),
        ],
        scratch_shapes=[
            pltpu.VMEM((KEYS, ROWS), jnp.float32),
            pltpu.VMEM((KEYS, PAIR), jnp.float32),
            pltpu.VMEM((KEYS, HEAD_SIZE), jnp.float32),
        ],
        compiler_params=pltpu.CompilerParams(vmem_limit_bytes=VMEM_LIMIT),
        name="probs_and_value_part",
    )(scalars, query, cotangent, kv)


def attention_grads(query, output, cotangent, kv, probs):
    return pl.pallas_call(
        grads_kernel,
        grid=(PAIRS,),
        in_specs=[
            pl.BlockSpec((ROWS, PAIR), pair_block),
            pl.BlockSpec((ROWS, PAIR), pair_block),
            pl.BlockSpec((ROWS, PAIR), pair_block),
            pl.BlockSpec((KEYS, 2 * HEAD_SIZE), whole),
            pl.BlockSpec((KEYS, PAIR), pair_block),
        ],
        out_specs=[
            pl.BlockSpec((ROWS, PAIR), pair_block),
            pl.BlockSpec((KEYS, HEAD_SIZE), whole),
        ],
        out_shape=[
            jax.ShapeDtypeStruct((ROWS, QUERY_HEADS * HEAD_SIZE), jnp.bfloat16),
            jax.ShapeDtypeStruct((KEYS, HEAD_SIZE), jnp.bfloat16),
        ],
        scratch_shapes=[
            pltpu.VMEM((HEAD_SIZE, KEYS), jnp.bfloat16),
            pltpu.VMEM((KEYS, HEAD_SIZE), jnp.float32),
            pltpu.VMEM((HEAD_SIZE, PAIR), jnp.float32),
        ],
        compiler_params=pltpu.CompilerParams(vmem_limit_bytes=VMEM_LIMIT),
        name="query_and_key_part",
    )(query, output, cotangent, kv, probs)


def exchange(blocks, axes):
    return lax.all_to_all(blocks, axes, 0, 0, tiled=False)


def gather(block, axes, count):
    return exchange(jnp.broadcast_to(block[None], (count,) + block.shape), axes)


def summed(blocks):
    return jnp.sum(blocks.astype(jnp.float32), axis=0)


def local(query, key, value, output, output_cotangent, inputs, doc_lengths, block_order):
    scalars = jnp.concatenate(
        [block_order, doc_lengths[0], lax.axis_index(CTX).astype(jnp.int32)[None]]
    )
    near_count, far_count = lax.axis_size(NEAR), lax.axis_size(FAR)
    low_count = lax.axis_size("ylo")
    columns = inputs.shape[1]
    kv = gather(jnp.concatenate([key[0], value[0]], axis=1), CTX, N_CTX).reshape(KEYS, -1)

    by_column_owner = inputs.reshape(ROWS, low_count, near_count, -1).transpose(2, 0, 1, 3)
    near_inputs = exchange(
        by_column_owner.reshape(near_count, ROWS, columns // near_count), NEAR
    ).reshape(near_count * ROWS, columns // near_count)

    probs, value_part = attention_probs(scalars, query[0], output_cotangent[0], kv)
    value_blocks = exchange(value_part.reshape(N_CTX, ROWS, HEAD_SIZE), CTX)
    query_grad, key_part = attention_grads(
        query[0], output[0], output_cotangent[0], kv, probs
    )
    value_grad = summed(value_blocks).astype(jnp.bfloat16)
    key_blocks = exchange(key_part.reshape(N_CTX, ROWS, HEAD_SIZE), CTX)
    key_grad = summed(key_blocks).astype(jnp.bfloat16)

    near_values = gather(value_grad, NEAR, near_count).reshape(-1, HEAD_SIZE)
    weight_part = lax.dot_general(
        near_inputs,
        near_values,
        (((0,), (0,)), ((), ())),
        preferred_element_type=jnp.float32,
    ).astype(jnp.bfloat16)
    weight_grad = summed(exchange(weight_part.reshape(far_count, -1, HEAD_SIZE), FAR))
    return query_grad[None], key_grad[None], value_grad[None], weight_grad


def solution(mesh):
    fine = Mesh(
        mesh.devices.reshape(2, 4, 2, 2, 8), ("ylo", "x", "core", "yhi", "z")
    )
    dp = ("ylo", "x", "core")
    tokens = P(dp, CTX, None)
    flat = P(dp + CTX, None)
    return jax.shard_map(
        local,
        mesh=fine,
        in_specs=(tokens,) * 5 + (flat, P(dp, None), P()),
        out_specs=(tokens, tokens, tokens, flat),
        check_vma=False,
    )
```

```python
import math

import jax
import jax.numpy as jnp
from jax import lax
from jax.experimental import pallas as pl
from jax.experimental.pallas import tpu as pltpu
from jax.sharding import Mesh, PartitionSpec as P

HEAD_SIZE = 128
QUERY_HEADS = 8
BLOCK = 64
BLOCKS = 32
NDOC = 8
ROWS = 128
KEYS = 2048
N_CTX = 16
CHUNK = 256
MOST = 1024
SPAN_BLOCKS = MOST // BLOCK + 1
SPAN = SPAN_BLOCKS * BLOCK
GROUP = 4
GROUPS = QUERY_HEADS // GROUP
LANES = GROUP * BLOCK
SCALE = HEAD_SIZE**-0.5
SCALE_LOG2 = SCALE * math.log2(math.e)
MASKED = -1e30
VMEM_LIMIT = 16 * 1024 * 1024
NT = (((1,), (1,)), ((), ()))

CTX = ("yhi", "z")
NEAR = ("x", "core")
FAR = ("ylo", "yhi", "z")


def chunks():
    return [(start, min(CHUNK, SPAN - start)) for start in range(0, SPAN, CHUNK)]


def fold_rows(tile, op):
    return op(tile.reshape(tile.shape[0] // 8, 8, tile.shape[1]), axis=0)


def heads_of(array, half, group):
    rows = slice(half * BLOCK, (half + 1) * BLOCK)
    first = group * GROUP
    return jnp.concatenate(
        [
            array[rows, (first + head) * HEAD_SIZE : (first + head + 1) * HEAD_SIZE]
            for head in range(GROUP)
        ],
        axis=0,
    )


def invert_order(scalars, slots):
    for slot in range(BLOCKS):
        slots[scalars[slot]] = slot


def span_of(scalars, half):
    own = scalars[2 * scalars[BLOCKS + NDOC] + half]
    start, end = jnp.int32(0), jnp.int32(0)
    for doc in range(NDOC):
        end = end + scalars[BLOCKS + doc]
        start = jnp.where(own * BLOCK >= end, end, start)
    return own, start // BLOCK


def slot_of(slots, first, step):
    return slots[jnp.minimum(first + step, BLOCKS - 1)]


def slot_rows(slots, first, step):
    return pl.ds(pl.multiple_of(slot_of(slots, first, step) * BLOCK, BLOCK), BLOCK)


def block_of(kv, part, slots, first, step):
    slot = slot_of(slots, first, step)
    rows = pl.ds(pl.multiple_of((slot % 2) * BLOCK, BLOCK), BLOCK)
    return kv[slot // 2, part, rows, :]


def write_bias(scalars, own, first, bias):
    lane = lax.broadcasted_iota(jnp.int32, (1, HEAD_SIZE), 1)
    high = own * BLOCK + lane % BLOCK
    low, end = jnp.zeros_like(high), jnp.int32(0)
    for doc in range(NDOC):
        end = end + scalars[BLOCKS + doc]
        low = jnp.where(high >= end, end, low)
    for start, size in chunks():
        row = lax.broadcasted_iota(jnp.int32, (size, HEAD_SIZE), 0)
        position = first * BLOCK + start + row
        allowed = (position <= high) & (position >= low)
        bias[start : start + size, :] = jnp.where(allowed, 0.0, MASKED)


def probs_kernel(
    scalars,
    query,
    cotangent,
    kv,
    probs,
    share_out,
    value_part,
    slots,
    keys,
    bias,
    scores,
    parts,
    low_parts,
    done,
):
    invert_order(scalars, slots)
    parts[...] = jnp.zeros_like(parts)
    for half in range(2):
        own, first = span_of(scalars, half)
        for step in range(SPAN_BLOCKS):
            keys[step * BLOCK : (step + 1) * BLOCK, :] = block_of(kv, 0, slots, first, step)
        write_bias(scalars, own, first, bias)
        for group in range(GROUPS):
            tile_index = half * GROUPS + group
            queries = heads_of(query, half, group)
            top = jnp.full((8, LANES), MASKED, jnp.float32)
            for start, size in chunks():
                rows = slice(start, start + size)
                raw = lax.dot_general(
                    keys[rows, :], queries, NT, preferred_element_type=jnp.float32
                )
                add = bias[rows, :]
                tile = raw * SCALE_LOG2 + jnp.concatenate([add, add], axis=1)
                scores[rows, :] = tile
                top = jnp.maximum(top, fold_rows(tile, jnp.max))
            top = jnp.max(top, axis=0, keepdims=True)
            total = jnp.zeros((8, LANES), jnp.float32)
            for start, size in chunks():
                rows = slice(start, start + size)
                tile = jnp.exp2(scores[rows, :] - top)
                probs[tile_index, rows, :] = tile.astype(jnp.bfloat16)
                total = total + fold_rows(tile, jnp.sum)
            share = 1.0 / jnp.sum(total, axis=0, keepdims=True)
            share_out[tile_index] = jnp.broadcast_to(share, (8, LANES))
        gradients = []
        for group in range(GROUPS):
            share = share_out[half * GROUPS + group][:1]
            by_row = jnp.broadcast_to(share, (HEAD_SIZE, LANES)).T
            gradients.append(
                (heads_of(cotangent, half, group).astype(jnp.float32) * by_row).astype(
                    jnp.bfloat16
                )
            )
        for start, size in chunks():
            rows = slice(start, start + size)
            add = sum(
                jnp.dot(
                    probs[half * GROUPS + group, rows, :],
                    gradients[group],
                    preferred_element_type=jnp.float32,
                )
                for group in range(GROUPS)
            )
            for step in range(size // BLOCK):
                target = slot_rows(slots, first, start // BLOCK + step)
                parts[target, :] += add[step * BLOCK : (step + 1) * BLOCK]
    low_parts[...] = parts[...].astype(jnp.bfloat16)
    copy = pltpu.make_async_copy(low_parts, value_part, done)
    copy.start()
    copy.wait()


def grads_kernel(
    scalars,
    query,
    output,
    cotangent,
    kv,
    probs,
    share_in,
    query_grad,
    key_sent,
    key_kept,
    slots,
    keys,
    values,
    key_turned,
    parts,
):
    invert_order(scalars, slots)
    parts[...] = jnp.zeros_like(parts)
    for half in range(2):
        _, first = span_of(scalars, half)
        for step in range(SPAN_BLOCKS):
            rows = slice(step * BLOCK, (step + 1) * BLOCK)
            keys[rows, :] = block_of(kv, 0, slots, first, step)
            values[rows, :] = block_of(kv, 1, slots, first, step)
        key_turned[...] = keys[...].T
        queries, gradients, deltas, shares, turned = [], [], [], [], []
        for group in range(GROUPS):
            queries.append(heads_of(query, half, group))
            gradients.append(heads_of(cotangent, half, group))
            product = gradients[group].astype(jnp.float32) * heads_of(output, half, group).astype(
                jnp.float32
            )
            deltas.append(jnp.sum(product.T, axis=0, keepdims=True))
            shares.append(share_in[half * GROUPS + group][:1])
            turned.append(jnp.zeros((HEAD_SIZE, LANES), jnp.float32))
        for start, size in chunks():
            rows = slice(start, start + size)
            add = 0.0
            for group in range(GROUPS):
                dprobs = lax.dot_general(
                    values[rows, :],
                    gradients[group],
                    NT,
                    preferred_element_type=jnp.float32,
                )
                weight = probs[half * GROUPS + group, rows, :].astype(jnp.float32) * shares[group]
                dscores = (weight * (dprobs - deltas[group])).astype(jnp.bfloat16)
                add = add + jnp.dot(dscores, queries[group], preferred_element_type=jnp.float32)
                turned[group] = turned[group] + jnp.dot(
                    key_turned[:, rows], dscores, preferred_element_type=jnp.float32
                )
            for step in range(size // BLOCK):
                target = slot_rows(slots, first, start // BLOCK + step)
                parts[target, :] += add[step * BLOCK : (step + 1) * BLOCK]
        for group in range(GROUPS):
            by_row = (turned[group] * SCALE).T.astype(jnp.bfloat16)
            for head in range(GROUP):
                column = (group * GROUP + head) * HEAD_SIZE
                query_grad[
                    half * BLOCK : (half + 1) * BLOCK, column : column + HEAD_SIZE
                ] = by_row[head * BLOCK : (head + 1) * BLOCK]
    me = scalars[BLOCKS + NDOC]
    for slot, relative in enumerate((0, 4, 2, 6, 1, 5, 3, 7)):
        for half, part in enumerate((key_kept, key_sent)):
            start = pl.multiple_of((me ^ (half * 8 + relative)) * ROWS, ROWS)
            part[slot] = (parts[pl.ds(start, ROWS), :] * SCALE).astype(part.dtype)


def attention_probs(scalars, query, cotangent, kv):
    return pl.pallas_call(
        probs_kernel,
        in_specs=[pl.BlockSpec(memory_space=pltpu.SMEM)]
        + [pl.BlockSpec(memory_space=pltpu.VMEM)] * 3,
        out_specs=[pl.BlockSpec(memory_space=pltpu.VMEM)] * 2
        + [pl.BlockSpec(memory_space=pltpu.HBM)],
        out_shape=[
            jax.ShapeDtypeStruct((2 * GROUPS, SPAN, LANES), jnp.bfloat16),
            jax.ShapeDtypeStruct((2 * GROUPS, 8, LANES), jnp.float32),
            jax.ShapeDtypeStruct((KEYS, HEAD_SIZE), jnp.bfloat16),
        ],
        scratch_shapes=[
            pltpu.SMEM((BLOCKS,), jnp.int32),
            pltpu.VMEM((SPAN, HEAD_SIZE), jnp.bfloat16),
            pltpu.VMEM((SPAN, HEAD_SIZE), jnp.float32),
            pltpu.VMEM((SPAN, LANES), jnp.float32),
            pltpu.VMEM((KEYS, HEAD_SIZE), jnp.float32),
            pltpu.VMEM((KEYS, HEAD_SIZE), jnp.bfloat16),
            pltpu.SemaphoreType.DMA,
        ],
        compiler_params=pltpu.CompilerParams(vmem_limit_bytes=VMEM_LIMIT),
        name="probs_and_value_part",
    )(scalars, query, cotangent, kv)


def attention_grads(scalars, query, output, cotangent, kv, probs, share):
    return pl.pallas_call(
        grads_kernel,
        in_specs=[pl.BlockSpec(memory_space=pltpu.SMEM)]
        + [pl.BlockSpec(memory_space=pltpu.VMEM)] * 6,
        out_specs=[pl.BlockSpec(memory_space=pltpu.VMEM)] * 3,
        out_shape=[
            jax.ShapeDtypeStruct((ROWS, QUERY_HEADS * HEAD_SIZE), jnp.bfloat16),
            jax.ShapeDtypeStruct((8, ROWS, HEAD_SIZE), jnp.bfloat16),
            jax.ShapeDtypeStruct((8, ROWS, HEAD_SIZE), jnp.float32),
        ],
        scratch_shapes=[
            pltpu.SMEM((BLOCKS,), jnp.int32),
            pltpu.VMEM((SPAN, HEAD_SIZE), jnp.bfloat16),
            pltpu.VMEM((SPAN, HEAD_SIZE), jnp.bfloat16),
            pltpu.VMEM((HEAD_SIZE, SPAN), jnp.bfloat16),
            pltpu.VMEM((KEYS, HEAD_SIZE), jnp.float32),
        ],
        compiler_params=pltpu.CompilerParams(vmem_limit_bytes=VMEM_LIMIT),
        name="query_and_key_part",
    )(scalars, query, output, cotangent, kv, probs, share)


def split_kernel(place, *refs):
    piece, parts = refs[0], refs[1:]
    step = pl.program_id(0)
    for relative in range(4):

        @pl.when(step // 4 == relative)
        def _(relative=relative):
            parts[relative][0] = piece[...]


def split_inputs(place, inputs):
    width = 512

    def source(step, place):
        relative, core, low = step // 4, (step // 2) % 2, step % 2
        near = (place[0] ^ relative) * 2 + (place[1] ^ core)
        return (0, low * 8 + near)

    def target(relative):
        def index(step, place):
            local_step = jnp.clip(step - 4 * relative, 0, 3)
            return (local_step // 2, 0, local_step % 2)

        return index

    return pl.pallas_call(
        split_kernel,
        grid_spec=pltpu.PrefetchScalarGridSpec(
            num_scalar_prefetch=1,
            grid=(16,),
            in_specs=[pl.BlockSpec((ROWS, width), source)],
            out_specs=[pl.BlockSpec((1, ROWS, width), target(r)) for r in range(4)],
        ),
        out_shape=[jax.ShapeDtypeStruct((2, ROWS, 2 * width), jnp.bfloat16)] * 4,
        name="split_inputs",
    )(place, inputs)


def stack_kernel(zero, one, two, three, after, stacked):
    for relative, piece in enumerate((zero, one, two, three)):
        stacked[relative] = piece[1]


def stack_partner(pieces, after):
    return pl.pallas_call(
        stack_kernel,
        in_specs=[pl.BlockSpec(memory_space=pltpu.VMEM)] * 4
        + [pl.BlockSpec(memory_space=pl.ANY)],
        out_specs=pl.BlockSpec(memory_space=pltpu.VMEM),
        out_shape=jax.ShapeDtypeStruct((4,) + pieces[0].shape[1:], jnp.bfloat16),
        compiler_params=pltpu.CompilerParams(vmem_limit_bytes=VMEM_LIMIT),
        name="stack_partner",
    )(*pieces, after)


def fold(kept, received, next_kept, next_sent):
    total = kept[...] + received[...].astype(jnp.float32)
    count = next_kept.shape[0]
    next_kept[...] = total[:count]
    next_sent[...] = total[count:].astype(jnp.bfloat16)


def halves_of(kept):
    half = (kept.shape[0] // 2,) + kept.shape[1:]
    return [
        jax.ShapeDtypeStruct(half, jnp.float32),
        jax.ShapeDtypeStruct(half, jnp.bfloat16),
    ]


def spread_kernel(blocks, kept, received, value_grad, spread, next_kept, next_sent):
    total = blocks[0].astype(jnp.float32)
    for block in range(1, blocks.shape[0]):
        total = total + blocks[block].astype(jnp.float32)
    low = total.astype(jnp.bfloat16)
    value_grad[...] = low
    for copy in range(spread.shape[0]):
        spread[copy] = low
    fold(kept, received, next_kept, next_sent)


def sum_and_spread(blocks, count, kept, received):
    shape = blocks.shape[1:]
    return pl.pallas_call(
        spread_kernel,
        in_specs=[pl.BlockSpec(memory_space=pltpu.VMEM)] * 3,
        out_specs=[pl.BlockSpec(memory_space=pltpu.VMEM)] * 4,
        out_shape=[
            jax.ShapeDtypeStruct(shape, jnp.bfloat16),
            jax.ShapeDtypeStruct((count,) + shape, jnp.bfloat16),
        ]
        + halves_of(kept),
        compiler_params=pltpu.CompilerParams(vmem_limit_bytes=VMEM_LIMIT),
        name="sum_and_spread",
    )(blocks, kept, received)


def join_kernel(key, value, joined, pair, done):
    pair[0] = key[...]
    pair[1] = value[...]
    copies = [
        pltpu.make_async_copy(pair, joined.at[copy], done.at[copy])
        for copy in range(joined.shape[0])
    ]
    for copy in copies:
        copy.start()
    for copy in copies:
        copy.wait()


def join_keys_values(key, value):
    return pl.pallas_call(
        join_kernel,
        in_specs=[pl.BlockSpec(memory_space=pltpu.VMEM)] * 2,
        out_specs=pl.BlockSpec(memory_space=pltpu.HBM),
        out_shape=jax.ShapeDtypeStruct((N_CTX, 2, ROWS, HEAD_SIZE), jnp.bfloat16),
        scratch_shapes=[
            pltpu.VMEM((2, ROWS, HEAD_SIZE), jnp.bfloat16),
            pltpu.SemaphoreType.DMA((N_CTX,)),
        ],
        name="join_keys_values",
    )(key, value)


def weight_kernel(
    place,
    values,
    own,
    one,
    two,
    three,
    partner,
    kept,
    received,
    weight_part,
    next_kept,
    next_sent,
):
    x, core = place[0], place[1]
    total = jnp.zeros((HEAD_SIZE, weight_part.shape[0]), jnp.float32)
    for relative, mine in enumerate((own, one, two, three)):
        near = (x ^ relative) * 2
        lhs = jnp.concatenate([values[near + core].T, values[near + (1 - core)].T], axis=1)
        rhs = jnp.concatenate([mine[0], partner[relative]], axis=0)
        total = total + jnp.dot(lhs, rhs, preferred_element_type=jnp.float32)
    for block in range(weight_part.shape[0] // HEAD_SIZE):
        columns = pl.ds(block * HEAD_SIZE, HEAD_SIZE)
        weight_part[columns, :] = total[:, block * HEAD_SIZE : (block + 1) * HEAD_SIZE].T.astype(
            jnp.bfloat16
        )
    fold(kept, received, next_kept, next_sent)


def weight_product(place, values, pieces, partner, kept, received):
    return pl.pallas_call(
        weight_kernel,
        in_specs=[pl.BlockSpec(memory_space=pltpu.SMEM)]
        + [pl.BlockSpec(memory_space=pltpu.VMEM)] * 8,
        out_specs=[pl.BlockSpec(memory_space=pltpu.VMEM)] * 3,
        out_shape=[jax.ShapeDtypeStruct((pieces[0].shape[2], HEAD_SIZE), jnp.bfloat16)]
        + halves_of(kept),
        compiler_params=pltpu.CompilerParams(vmem_limit_bytes=VMEM_LIMIT),
        name="weight_product",
    )(place, values, *pieces, partner, kept, received)


def exchange(blocks, axes):
    return lax.all_to_all(blocks, axes, 0, 0, tiled=False)


def summed(blocks):
    return jnp.sum(blocks.astype(jnp.float32), axis=0)


def swapped(block, axis, shift):
    count = lax.axis_size(axis)
    return lax.ppermute(block, axis, [(i, i ^ shift) for i in range(count)])


def local(query, key, value, output, output_cotangent, inputs, doc_lengths, block_order):
    scalars = jnp.concatenate(
        [block_order, doc_lengths[0], lax.axis_index(CTX).astype(jnp.int32)[None]]
    )
    place = jnp.stack([lax.axis_index("x"), lax.axis_index("core")]).astype(jnp.int32)
    near_count, far_count = lax.axis_size(NEAR), lax.axis_size(FAR)
    kv = exchange(join_keys_values(key[0], value[0]), CTX)

    parts = split_inputs(place, inputs)
    pieces = [parts[0]] + [swapped(parts[r], "x", r) for r in range(1, 4)]
    probs, share, value_part = attention_probs(scalars, query[0], output_cotangent[0], kv)
    value_blocks = exchange(value_part.reshape(N_CTX, ROWS, HEAD_SIZE), CTX)
    query_grad, key_sent, key_kept = attention_grads(
        scalars, query[0], output[0], output_cotangent[0], kv, probs, share
    )
    partner = swapped(stack_partner(pieces, query_grad), "core", 1)
    value_grad, spread, key_kept, key_sent = sum_and_spread(
        value_blocks, near_count, key_kept, swapped(key_sent, "yhi", 1)
    )
    near_values = exchange(spread, NEAR)
    weight_part, key_kept, key_sent = weight_product(
        place, near_values, pieces, partner, key_kept, swapped(key_sent, "z", 1)
    )
    weight_blocks = exchange(weight_part.reshape(far_count, -1, HEAD_SIZE), FAR)
    key_sum = key_kept + swapped(key_sent, "z", 2).astype(jnp.float32)
    received = swapped(key_sum[1:].astype(jnp.bfloat16), "z", 4)
    key_grad = (key_sum[:1] + received.astype(jnp.float32)).astype(jnp.bfloat16)
    weight_grad = summed(weight_blocks)
    return query_grad[None], key_grad, value_grad[None], weight_grad


def solution(mesh):
    fine = Mesh(
        mesh.devices.reshape(2, 4, 2, 2, 8), ("ylo", "x", "core", "yhi", "z")
    )
    dp = ("ylo", "x", "core")
    tokens = P(dp, CTX, None)
    flat = P(dp + CTX, None)
    return jax.shard_map(
        local,
        mesh=fine,
        in_specs=(tokens,) * 5 + (flat, P(dp, None), P()),
        out_specs=(tokens, tokens, tokens, flat),
        check_vma=False,
    )
```

```python
import math

import jax
import jax.numpy as jnp
from jax import lax
from jax.experimental import pallas as pl
from jax.experimental.pallas import tpu as pltpu
from jax.sharding import Mesh, PartitionSpec as P

HEAD_SIZE = 128
QUERY_HEADS = 8
BLOCK = 64
BLOCKS = 32
NDOC = 8
ROWS = 128
KEYS = 2048
N_CTX = 16
CHUNK = 256
MOST = 1024
SPAN_BLOCKS = MOST // BLOCK + 1
SPAN = SPAN_BLOCKS * BLOCK
GROUP = 4
GROUPS = QUERY_HEADS // GROUP
LANES = GROUP * BLOCK
SCALE = HEAD_SIZE**-0.5
SCALE_LOG2 = SCALE * math.log2(math.e)
MASKED = -1e30
WIDTH = 512
VMEM_LIMIT = 16 * 1024 * 1024
NT = (((1,), (1,)), ((), ()))

CTX = ("yhi", "z")
NEAR = ("x", "core")
FAR = ("ylo", "yhi", "z")


def chunks():
    return [(start, min(CHUNK, SPAN - start)) for start in range(0, SPAN, CHUNK)]


def fold_rows(tile, op):
    return op(tile.reshape(tile.shape[0] // 8, 8, tile.shape[1]), axis=0)


def heads_of(array, half, group):
    rows = slice(half * BLOCK, (half + 1) * BLOCK)
    first = group * GROUP
    return jnp.concatenate(
        [
            array[rows, (first + head) * HEAD_SIZE : (first + head + 1) * HEAD_SIZE]
            for head in range(GROUP)
        ],
        axis=0,
    )


def invert_order(scalars, slots):
    for slot in range(BLOCKS):
        slots[scalars[slot]] = slot


def span_of(scalars, half):
    own = scalars[2 * scalars[BLOCKS + NDOC] + half]
    start, end = jnp.int32(0), jnp.int32(0)
    for doc in range(NDOC):
        end = end + scalars[BLOCKS + doc]
        start = jnp.where(own * BLOCK >= end, end, start)
    return own, start // BLOCK


def slot_of(slots, first, step):
    return slots[jnp.minimum(first + step, BLOCKS - 1)]


def slot_rows(slots, first, step):
    return pl.ds(pl.multiple_of(slot_of(slots, first, step) * BLOCK, BLOCK), BLOCK)


def key_block(kv, slots, first, step):
    slot = slot_of(slots, first, step)
    rows = pl.ds(pl.multiple_of((slot % 2) * BLOCK, BLOCK), BLOCK)
    return kv[slot // 2, rows, :]


def value_block(kv, far_values, slots, first, step, half):
    slot = slot_of(slots, first, step)
    return jnp.where(slot % 2 == half, kv[slot // 2, ROWS:, :], far_values[slot // 2])


def write_bias(scalars, own, first, bias):
    lane = lax.broadcasted_iota(jnp.int32, (1, HEAD_SIZE), 1)
    high = own * BLOCK + lane % BLOCK
    low, end = jnp.zeros_like(high), jnp.int32(0)
    for doc in range(NDOC):
        end = end + scalars[BLOCKS + doc]
        low = jnp.where(high >= end, end, low)
    for start, size in chunks():
        row = lax.broadcasted_iota(jnp.int32, (size, HEAD_SIZE), 0)
        position = first * BLOCK + start + row
        allowed = (position <= high) & (position >= low)
        bias[start : start + size, :] = jnp.where(allowed, 0.0, MASKED)


def probs_kernel(
    scalars,
    query,
    cotangent,
    kv,
    probs,
    value_part,
    slots,
    keys,
    bias,
    scores,
    parts,
    low_parts,
    queries_in,
    gradients_in,
    done,
):
    fetches = [
        pltpu.make_async_copy(query, queries_in, done.at[0]),
        pltpu.make_async_copy(cotangent, gradients_in, done.at[1]),
    ]
    for copy in fetches:
        copy.start()
    invert_order(scalars, slots)
    parts[...] = jnp.zeros_like(parts)
    for half in range(2):
        own, first = span_of(scalars, half)
        for step in range(SPAN_BLOCKS):
            keys[step * BLOCK : (step + 1) * BLOCK, :] = key_block(kv, slots, first, step)
        write_bias(scalars, own, first, bias)
        if half == 0:
            fetches[0].wait()
        shares = []
        for group in range(GROUPS):
            tile_index = half * GROUPS + group
            queries = heads_of(queries_in, half, group)
            top = jnp.full((8, LANES), MASKED, jnp.float32)
            for start, size in chunks():
                rows = slice(start, start + size)
                raw = lax.dot_general(
                    keys[rows, :], queries, NT, preferred_element_type=jnp.float32
                )
                add = bias[rows, :]
                tile = raw * SCALE_LOG2 + jnp.concatenate([add, add], axis=1)
                scores[rows, :] = tile
                top = jnp.maximum(top, fold_rows(tile, jnp.max))
            top = jnp.max(top, axis=0, keepdims=True)
            total = jnp.zeros((8, LANES), jnp.float32)
            for start, size in chunks():
                rows = slice(start, start + size)
                tile = jnp.exp2(scores[rows, :] - top)
                probs[tile_index, rows, :] = tile.astype(jnp.bfloat16)
                total = total + fold_rows(tile, jnp.sum)
            share = 1.0 / jnp.sum(total, axis=0, keepdims=True)
            shares.append(share)
            share = jnp.broadcast_to(share, (8, LANES))
            coarse = share.astype(jnp.bfloat16)
            rest = (share - coarse.astype(jnp.float32)).astype(jnp.bfloat16)
            probs[tile_index, SPAN:, :] = jnp.concatenate([coarse, rest], axis=0)
        if half == 0:
            fetches[1].wait()
        gradients = []
        for group in range(GROUPS):
            by_row = jnp.broadcast_to(shares[group], (HEAD_SIZE, LANES)).T
            gradients.append(
                (heads_of(gradients_in, half, group).astype(jnp.float32) * by_row).astype(
                    jnp.bfloat16
                )
            )
        for start, size in chunks():
            rows = slice(start, start + size)
            add = sum(
                jnp.dot(
                    probs[half * GROUPS + group, rows, :],
                    gradients[group],
                    preferred_element_type=jnp.float32,
                )
                for group in range(GROUPS)
            )
            for step in range(size // BLOCK):
                target = slot_rows(slots, first, start // BLOCK + step)
                parts[target, :] += add[step * BLOCK : (step + 1) * BLOCK]
    low_parts[...] = parts[...].astype(jnp.bfloat16)
    copy = pltpu.make_async_copy(low_parts, value_part, done.at[2])
    copy.start()
    copy.wait()


def grads_kernel(
    scalars,
    query,
    output,
    cotangent,
    kv,
    far_values,
    probs,
    query_grad,
    key_sent,
    key_kept,
    slots,
    keys,
    values,
    key_turned,
    parts,
    queries_in,
    output_in,
    gradients_in,
    done,
):
    fetches = [
        pltpu.make_async_copy(source, target, done.at[index])
        for index, (source, target) in enumerate(
            ((cotangent, gradients_in), (output, output_in), (query, queries_in))
        )
    ]
    for copy in fetches:
        copy.start()
    me = scalars[BLOCKS + NDOC]
    invert_order(scalars, slots)
    parts[...] = jnp.zeros_like(parts)
    for half in range(2):
        _, first = span_of(scalars, half)
        for step in range(SPAN_BLOCKS):
            rows = slice(step * BLOCK, (step + 1) * BLOCK)
            keys[rows, :] = key_block(kv, slots, first, step)
            values[rows, :] = value_block(kv, far_values, slots, first, step, me // 8)
        key_turned[...] = keys[...].T
        if half == 0:
            for copy in fetches:
                copy.wait()
        queries, gradients, deltas, shares, turned = [], [], [], [], []
        for group in range(GROUPS):
            queries.append(heads_of(queries_in, half, group))
            gradients.append(heads_of(gradients_in, half, group))
            forward = heads_of(output_in, half, group).astype(jnp.float32)
            product = gradients[group].astype(jnp.float32) * forward
            deltas.append(jnp.sum(product.T, axis=0, keepdims=True))
            pieces = probs[half * GROUPS + group, SPAN:, :].astype(jnp.float32)
            shares.append(pieces[:1] + pieces[8:9])
            turned.append(jnp.zeros((HEAD_SIZE, LANES), jnp.float32))
        for start, size in chunks():
            rows = slice(start, start + size)
            add = 0.0
            for group in range(GROUPS):
                dprobs = lax.dot_general(
                    values[rows, :],
                    gradients[group],
                    NT,
                    preferred_element_type=jnp.float32,
                )
                weight = probs[half * GROUPS + group, rows, :].astype(jnp.float32) * shares[group]
                dscores = (weight * (dprobs - deltas[group])).astype(jnp.bfloat16)
                add = add + jnp.dot(dscores, queries[group], preferred_element_type=jnp.float32)
                turned[group] = turned[group] + jnp.dot(
                    key_turned[:, rows], dscores, preferred_element_type=jnp.float32
                )
            for step in range(size // BLOCK):
                target = slot_rows(slots, first, start // BLOCK + step)
                parts[target, :] += add[step * BLOCK : (step + 1) * BLOCK]
        for group in range(GROUPS):
            by_row = (turned[group] * SCALE).T.astype(jnp.bfloat16)
            for head in range(GROUP):
                column = (group * GROUP + head) * HEAD_SIZE
                query_grad[
                    half * BLOCK : (half + 1) * BLOCK, column : column + HEAD_SIZE
                ] = by_row[head * BLOCK : (head + 1) * BLOCK]
    for slot, relative in enumerate((0, 7, 2, 5, 1, 6, 3, 4)):
        for half, part in enumerate((key_kept, key_sent)):
            start = pl.multiple_of((me ^ (half * 8 + relative)) * ROWS, ROWS)
            part[slot] = (parts[pl.ds(start, ROWS), :] * SCALE).astype(part.dtype)


def in_vmem(array):
    return pltpu.with_memory_space_constraint(array, pltpu.VMEM)


def in_hbm(array):
    return pltpu.with_memory_space_constraint(array, pltpu.HBM)


VMEM_SPEC = pl.BlockSpec(memory_space=pltpu.VMEM)
HBM_SPEC = pl.BlockSpec(memory_space=pltpu.HBM)
SMEM_SPEC = pl.BlockSpec(memory_space=pltpu.SMEM)
PARAMS = pltpu.CompilerParams(vmem_limit_bytes=VMEM_LIMIT)


def attention_probs(scalars, query, cotangent, kv):
    return pl.pallas_call(
        probs_kernel,
        in_specs=[SMEM_SPEC, HBM_SPEC, HBM_SPEC, VMEM_SPEC],
        out_specs=[VMEM_SPEC, HBM_SPEC],
        out_shape=[
            jax.ShapeDtypeStruct((2 * GROUPS, SPAN + 16, LANES), jnp.bfloat16),
            pltpu.HBM((KEYS, HEAD_SIZE), jnp.bfloat16),
        ],
        scratch_shapes=[
            pltpu.SMEM((BLOCKS,), jnp.int32),
            pltpu.VMEM((SPAN, HEAD_SIZE), jnp.bfloat16),
            pltpu.VMEM((SPAN, HEAD_SIZE), jnp.float32),
            pltpu.VMEM((SPAN, LANES), jnp.float32),
            pltpu.VMEM((KEYS, HEAD_SIZE), jnp.float32),
            pltpu.VMEM((KEYS, HEAD_SIZE), jnp.bfloat16),
            pltpu.VMEM((ROWS, QUERY_HEADS * HEAD_SIZE), jnp.bfloat16),
            pltpu.VMEM((ROWS, QUERY_HEADS * HEAD_SIZE), jnp.bfloat16),
            pltpu.SemaphoreType.DMA((3,)),
        ],
        compiler_params=PARAMS,
        name="probs_and_value_part",
    )(scalars, in_hbm(query), in_hbm(cotangent), kv)


def attention_grads(scalars, query, output, cotangent, kv, far_values, probs):
    return pl.pallas_call(
        grads_kernel,
        in_specs=[SMEM_SPEC] + [HBM_SPEC] * 3 + [VMEM_SPEC] * 3,
        out_specs=[VMEM_SPEC] * 3,
        out_shape=[
            jax.ShapeDtypeStruct((ROWS, QUERY_HEADS * HEAD_SIZE), jnp.bfloat16),
            jax.ShapeDtypeStruct((8, ROWS, HEAD_SIZE), jnp.bfloat16),
            jax.ShapeDtypeStruct((8, ROWS, HEAD_SIZE), jnp.float32),
        ],
        scratch_shapes=[
            pltpu.SMEM((BLOCKS,), jnp.int32),
            pltpu.VMEM((SPAN, HEAD_SIZE), jnp.bfloat16),
            pltpu.VMEM((SPAN, HEAD_SIZE), jnp.bfloat16),
            pltpu.VMEM((HEAD_SIZE, SPAN), jnp.bfloat16),
            pltpu.VMEM((KEYS, HEAD_SIZE), jnp.float32),
            pltpu.VMEM((ROWS, QUERY_HEADS * HEAD_SIZE), jnp.bfloat16),
            pltpu.VMEM((ROWS, QUERY_HEADS * HEAD_SIZE), jnp.bfloat16),
            pltpu.VMEM((ROWS, QUERY_HEADS * HEAD_SIZE), jnp.bfloat16),
            pltpu.SemaphoreType.DMA((3,)),
        ],
        compiler_params=PARAMS,
        name="query_and_key_part",
    )(scalars, *map(in_hbm, (query, output, cotangent)), kv, far_values, probs)


def stack_kernel(zero, one, two, three, after, stacked, staged, done):
    fetches = [
        pltpu.make_async_copy(piece.at[1], staged.at[relative], done.at[relative])
        for relative, piece in enumerate((zero, one, two, three))
    ]
    stores = [
        pltpu.make_async_copy(staged.at[relative], stacked.at[relative], done.at[relative])
        for relative in range(4)
    ]
    for copy in fetches:
        copy.start()
    for copy, store in zip(fetches, stores):
        copy.wait()
        store.start()
    for store in stores:
        store.wait()


def stack_partner(pieces, after):
    shape = (4,) + pieces[0].shape[1:]
    return pl.pallas_call(
        stack_kernel,
        in_specs=[HBM_SPEC] * 5,
        out_specs=HBM_SPEC,
        out_shape=pltpu.HBM(shape, jnp.bfloat16),
        scratch_shapes=[pltpu.VMEM(shape, jnp.bfloat16), pltpu.SemaphoreType.DMA((4,))],
        compiler_params=PARAMS,
        name="stack_partner",
    )(*map(in_hbm, pieces), in_hbm(after))


def load_kernel(zero, one, two, three, partner, sources, done):
    copies = []
    for relative, mine in enumerate((zero, one, two, three)):
        for other, source in enumerate((mine.at[0], partner.at[relative])):
            target = sources.at[relative, pl.ds(other * ROWS, ROWS), :]
            copies.append(pltpu.make_async_copy(source, target, done.at[2 * relative + other]))
    for copy in copies:
        copy.start()
    for copy in copies:
        copy.wait()


def load_inputs(pieces, partner):
    return pl.pallas_call(
        load_kernel,
        in_specs=[HBM_SPEC] * 5,
        out_specs=VMEM_SPEC,
        out_shape=pltpu.VMEM((4, 2 * ROWS, pieces[0].shape[2]), jnp.bfloat16),
        scratch_shapes=[pltpu.SemaphoreType.DMA((8,))],
        compiler_params=PARAMS,
        name="load_inputs",
    )(*map(in_hbm, pieces), in_hbm(partner))


def split_kernel(place, inputs, zero, one, two, three, staged, done):
    x, core = place[0], place[1]
    fetches, stores = [], []
    for relative, part in enumerate((zero, one, two, three)):
        for other in range(2):
            index = 2 * relative + other
            near = (x ^ relative) * 2 + (core ^ other)
            for low in range(2):
                start = pl.multiple_of((low * 8 + near) * WIDTH, WIDTH)
                fetches.append(
                    pltpu.make_async_copy(
                        inputs.at[:, pl.ds(start, WIDTH)],
                        staged.at[index, :, pl.ds(low * WIDTH, WIDTH)],
                        done.at[2 * index + low],
                    )
                )
            stores.append(
                pltpu.make_async_copy(staged.at[index], part.at[other], done.at[2 * index])
            )
    for copy in fetches:
        copy.start()
    for index, store in enumerate(stores):
        fetches[2 * index].wait()
        fetches[2 * index + 1].wait()
        store.start()
    for store in stores:
        store.wait()


def split_inputs(place, inputs):
    return pl.pallas_call(
        split_kernel,
        in_specs=[SMEM_SPEC, HBM_SPEC],
        out_specs=[HBM_SPEC] * 4,
        out_shape=[pltpu.HBM((2, ROWS, 2 * WIDTH), jnp.bfloat16)] * 4,
        scratch_shapes=[
            pltpu.VMEM((8, ROWS, 2 * WIDTH), jnp.bfloat16),
            pltpu.SemaphoreType.DMA((16,)),
        ],
        compiler_params=PARAMS,
        name="split_inputs",
    )(place, in_hbm(inputs))


def fold(kept, received, next_kept, next_sent):
    total = kept[...] + received[...].astype(jnp.float32)
    count = next_kept.shape[0]
    next_kept[...] = total[:count]
    next_sent[...] = total[count:].astype(jnp.bfloat16)


def halves_of(kept):
    half = (kept.shape[0] // 2,) + kept.shape[1:]
    return [
        jax.ShapeDtypeStruct(half, jnp.float32),
        jax.ShapeDtypeStruct(half, jnp.bfloat16),
    ]


def spread_kernel(
    blocks, kept, received, value_grad, spread, next_kept, next_sent, arrived, low, old, done
):
    count = blocks.shape[0]
    fetches = [
        pltpu.make_async_copy(blocks.at[block], arrived.at[block], done.at[block])
        for block in range(count)
    ]
    fetch_old = pltpu.make_async_copy(kept, old, done.at[count])
    for copy in fetches + [fetch_old]:
        copy.start()
    total = 0.0
    for block in range(count):
        fetches[block].wait()
        total = total + arrived[block].astype(jnp.float32)
    low[...] = total.astype(jnp.bfloat16)
    value_grad[...] = low[...]
    stores = [
        pltpu.make_async_copy(low, spread.at[copy], done.at[copy])
        for copy in range(spread.shape[0])
    ]
    for copy in stores:
        copy.start()
    fetch_old.wait()
    fold(old, received, next_kept, next_sent)
    for copy in stores:
        copy.wait()


def sum_and_spread(blocks, count, kept, received):
    shape = blocks.shape[1:]
    return pl.pallas_call(
        spread_kernel,
        in_specs=[HBM_SPEC, HBM_SPEC, VMEM_SPEC],
        out_specs=[VMEM_SPEC, HBM_SPEC, VMEM_SPEC, VMEM_SPEC],
        out_shape=[
            jax.ShapeDtypeStruct(shape, jnp.bfloat16),
            pltpu.HBM((count,) + shape, jnp.bfloat16),
        ]
        + halves_of(kept),
        scratch_shapes=[
            pltpu.VMEM(blocks.shape, jnp.bfloat16),
            pltpu.VMEM(shape, jnp.bfloat16),
            pltpu.VMEM(kept.shape, jnp.float32),
            pltpu.SemaphoreType.DMA((blocks.shape[0] + 1,)),
        ],
        compiler_params=PARAMS,
        name="sum_and_spread",
    )(in_hbm(blocks), in_hbm(kept), received)


def join_kernel(key, value, joined, both, done):
    copies = []
    for half in range(2):
        both[half, :ROWS] = key[...]
        both[half, ROWS:] = value[half * BLOCK : (half + 1) * BLOCK]
        for copy in range(half * N_CTX // 2, (half + 1) * N_CTX // 2):
            copies.append(pltpu.make_async_copy(both.at[half], joined.at[copy], done.at[copy]))
            copies[-1].start()
    for copy in copies:
        copy.wait()


def join_keys_values(key, value):
    return pl.pallas_call(
        join_kernel,
        in_specs=[VMEM_SPEC] * 2,
        out_specs=HBM_SPEC,
        out_shape=pltpu.HBM((N_CTX, ROWS + BLOCK, HEAD_SIZE), jnp.bfloat16),
        scratch_shapes=[
            pltpu.VMEM((2, ROWS + BLOCK, HEAD_SIZE), jnp.bfloat16),
            pltpu.SemaphoreType.DMA((N_CTX,)),
        ],
        name="join_keys_values",
    )(key, value)


def weight_kernel(place, values, sources, kept, received, weight_part, next_kept, next_sent):
    x, core = place[0], place[1]
    total = 0.0
    for relative in range(4):
        near = (x ^ relative) * 2
        lhs = jnp.concatenate([values[near + core].T, values[near + (1 - core)].T], axis=1)
        total = total + jnp.dot(lhs, sources[relative], preferred_element_type=jnp.float32)
    for block in range(weight_part.shape[0] // HEAD_SIZE):
        columns = pl.ds(block * HEAD_SIZE, HEAD_SIZE)
        weight_part[columns, :] = total[:, block * HEAD_SIZE : (block + 1) * HEAD_SIZE].T.astype(
            jnp.bfloat16
        )
    fold(kept, received, next_kept, next_sent)


def weight_product(place, values, sources, kept, received):
    return pl.pallas_call(
        weight_kernel,
        in_specs=[SMEM_SPEC] + [VMEM_SPEC] * 4,
        out_specs=[VMEM_SPEC] * 3,
        out_shape=[jax.ShapeDtypeStruct((2 * WIDTH, HEAD_SIZE), jnp.bfloat16)] + halves_of(kept),
        compiler_params=PARAMS,
        name="weight_product",
    )(place, values, in_vmem(sources), kept, received)


def exchange(blocks, axes):
    return lax.all_to_all(blocks, axes, 0, 0, tiled=False)


def summed(blocks):
    return jnp.sum(blocks.astype(jnp.float32), axis=0)


def swapped(block, axis, shift):
    count = lax.axis_size(axis)
    return lax.ppermute(block, axis, [(i, i ^ shift) for i in range(count)])


def local(query, key, value, output, output_cotangent, inputs, doc_lengths, block_order):
    scalars = jnp.concatenate(
        [block_order, doc_lengths[0], lax.axis_index(CTX).astype(jnp.int32)[None]]
    )
    place = jnp.stack([lax.axis_index("x"), lax.axis_index("core")]).astype(jnp.int32)
    near_count, far_count = lax.axis_size(NEAR), lax.axis_size(FAR)
    kv = exchange(join_keys_values(key[0], value[0]), CTX)
    far_values = swapped(kv[:, ROWS:], "yhi", 1)

    parts = split_inputs(place, inputs)
    pieces = [parts[0]] + [swapped(parts[r], "x", r) for r in range(1, 4)]
    probs, value_part = attention_probs(scalars, query[0], output_cotangent[0], kv)
    value_blocks = exchange(value_part.reshape(N_CTX, ROWS, HEAD_SIZE), CTX)
    query_grad, key_sent, key_kept = attention_grads(
        scalars, query[0], output[0], output_cotangent[0], kv, far_values, probs
    )
    partner = swapped(stack_partner(pieces, key_kept), "core", 1)
    sources = load_inputs(pieces, partner)
    value_grad, spread, key_kept, key_sent = sum_and_spread(
        value_blocks, near_count, key_kept, swapped(key_sent, "yhi", 1)
    )
    near_values = exchange(spread, NEAR)
    weight_part, key_kept, key_sent = weight_product(
        place, near_values, sources, key_kept, swapped(key_sent, "z", 1)
    )
    weight_blocks = exchange(weight_part.reshape(far_count, -1, HEAD_SIZE), FAR)
    key_sum = key_kept + swapped(key_sent, "z", 2).astype(jnp.float32)
    received = swapped(key_sum[1:].astype(jnp.bfloat16), "z", 7)
    key_grad = (key_sum[:1] + received.astype(jnp.float32)).astype(jnp.bfloat16)
    weight_grad = summed(weight_blocks)
    return query_grad[None], key_grad, value_grad[None], weight_grad


def solution(mesh):
    fine = Mesh(
        mesh.devices.reshape(2, 4, 2, 2, 8), ("ylo", "x", "core", "yhi", "z")
    )
    dp = ("ylo", "x", "core")
    tokens = P(dp, CTX, None)
    flat = P(dp + CTX, None)
    return jax.shard_map(
        local,
        mesh=fine,
        in_specs=(tokens,) * 5 + (flat, P(dp, None), P()),
        out_specs=(tokens, tokens, tokens, flat),
        check_vma=False,
    )
```

```python
import math

import jax
import jax.numpy as jnp
from jax import lax
from jax.experimental import pallas as pl
from jax.experimental.pallas import tpu as pltpu
from jax.sharding import Mesh, PartitionSpec as P

HEAD_SIZE = 128
QUERY_HEADS = 8
BLOCK = 64
BLOCKS = 32
NDOC = 8
ROWS = 128
KEYS = 2048
N_CTX = 16
CHUNK = 256
MOST = 1024
SPAN_BLOCKS = MOST // BLOCK + 1
SPAN = SPAN_BLOCKS * BLOCK
GROUP = 4
GROUPS = QUERY_HEADS // GROUP
LANES = GROUP * BLOCK
SCALE = HEAD_SIZE**-0.5
SCALE_LOG2 = SCALE * math.log2(math.e)
MASKED = -1e30
WIDTH = 512
VMEM_LIMIT = 16 * 1024 * 1024
NT = (((1,), (1,)), ((), ()))

CTX = ("yhi", "z")
NEAR = ("x", "core")
FAR = ("ylo", "yhi", "z")


def chunks():
    return [(start, min(CHUNK, SPAN - start)) for start in range(0, SPAN, CHUNK)]


def fold_rows(tile, op):
    return op(tile.reshape(tile.shape[0] // 8, 8, tile.shape[1]), axis=0)


def heads_of(array, half, group):
    rows = slice(half * BLOCK, (half + 1) * BLOCK)
    first = group * GROUP
    return jnp.concatenate(
        [
            array[rows, (first + head) * HEAD_SIZE : (first + head + 1) * HEAD_SIZE]
            for head in range(GROUP)
        ],
        axis=0,
    )


def invert_order(scalars, slots):
    for slot in range(BLOCKS):
        slots[scalars[slot]] = slot


def span_of(scalars, half):
    own = scalars[2 * scalars[BLOCKS + NDOC] + half]
    start, end = jnp.int32(0), jnp.int32(0)
    for doc in range(NDOC):
        end = end + scalars[BLOCKS + doc]
        start = jnp.where(own * BLOCK >= end, end, start)
    return own, start // BLOCK


def slot_of(slots, first, step):
    return slots[jnp.minimum(first + step, BLOCKS - 1)]


def slot_rows(slots, first, step):
    return pl.ds(pl.multiple_of(slot_of(slots, first, step) * BLOCK, BLOCK), BLOCK)


def key_block(kv, slots, first, step):
    slot = slot_of(slots, first, step)
    rows = pl.ds(pl.multiple_of((slot % 2) * BLOCK, BLOCK), BLOCK)
    return kv[slot // 2, rows, :]


def value_block(kv, far_values, slots, first, step, half):
    slot = slot_of(slots, first, step)
    return jnp.where(slot % 2 == half, kv[slot // 2, ROWS:, :], far_values[slot // 2])


def write_bias(scalars, own, first, bias):
    lane = lax.broadcasted_iota(jnp.int32, (1, HEAD_SIZE), 1)
    high = own * BLOCK + lane % BLOCK
    low, end = jnp.zeros_like(high), jnp.int32(0)
    for doc in range(NDOC):
        end = end + scalars[BLOCKS + doc]
        low = jnp.where(high >= end, end, low)
    for start, size in chunks():
        row = lax.broadcasted_iota(jnp.int32, (size, HEAD_SIZE), 0)
        position = first * BLOCK + start + row
        allowed = (position <= high) & (position >= low)
        bias[start : start + size, :] = jnp.where(allowed, 0.0, MASKED)


def probs_kernel(
    scalars,
    query,
    cotangent,
    kv,
    probs,
    value_part,
    slots,
    keys,
    bias,
    scores,
    parts,
    low_parts,
    queries_in,
    gradients_in,
    done,
):
    fetches = [
        pltpu.make_async_copy(query, queries_in, done.at[0]),
        pltpu.make_async_copy(cotangent, gradients_in, done.at[1]),
    ]
    for copy in fetches:
        copy.start()
    invert_order(scalars, slots)
    parts[...] = jnp.zeros_like(parts)
    for half in range(2):
        own, first = span_of(scalars, half)
        for step in range(SPAN_BLOCKS):
            keys[step * BLOCK : (step + 1) * BLOCK, :] = key_block(kv, slots, first, step)
        write_bias(scalars, own, first, bias)
        if half == 0:
            fetches[0].wait()
        shares = []
        for group in range(GROUPS):
            tile_index = half * GROUPS + group
            queries = heads_of(queries_in, half, group)
            top = jnp.full((8, LANES), MASKED, jnp.float32)
            for start, size in chunks():
                rows = slice(start, start + size)
                raw = lax.dot_general(
                    keys[rows, :], queries, NT, preferred_element_type=jnp.float32
                )
                add = bias[rows, :]
                tile = raw * SCALE_LOG2 + jnp.concatenate([add, add], axis=1)
                scores[rows, :] = tile
                top = jnp.maximum(top, fold_rows(tile, jnp.max))
            top = jnp.max(top, axis=0, keepdims=True)
            total = jnp.zeros((8, LANES), jnp.float32)
            for start, size in chunks():
                rows = slice(start, start + size)
                tile = jnp.exp2(scores[rows, :] - top)
                probs[tile_index, rows, :] = tile.astype(jnp.bfloat16)
                total = total + fold_rows(tile, jnp.sum)
            share = 1.0 / jnp.sum(total, axis=0, keepdims=True)
            shares.append(share)
            share = jnp.broadcast_to(share, (8, LANES))
            coarse = share.astype(jnp.bfloat16)
            rest = (share - coarse.astype(jnp.float32)).astype(jnp.bfloat16)
            probs[tile_index, SPAN:, :] = jnp.concatenate([coarse, rest], axis=0)
        if half == 0:
            fetches[1].wait()
        gradients = []
        for group in range(GROUPS):
            by_row = jnp.broadcast_to(shares[group], (HEAD_SIZE, LANES)).T
            gradients.append(
                (heads_of(gradients_in, half, group).astype(jnp.float32) * by_row).astype(
                    jnp.bfloat16
                )
            )
        for start, size in chunks():
            rows = slice(start, start + size)
            add = sum(
                jnp.dot(
                    probs[half * GROUPS + group, rows, :],
                    gradients[group],
                    preferred_element_type=jnp.float32,
                )
                for group in range(GROUPS)
            )
            for step in range(size // BLOCK):
                target = slot_rows(slots, first, start // BLOCK + step)
                parts[target, :] += add[step * BLOCK : (step + 1) * BLOCK]
    copies = []
    for piece in range(4):
        rows = pl.ds(piece * KEYS // 4, KEYS // 4)
        low_parts[rows, :] = parts[rows, :].astype(jnp.bfloat16)
        copies.append(
            pltpu.make_async_copy(
                low_parts.at[rows, :], value_part.at[rows, :], done.at[2 + piece]
            )
        )
        copies[-1].start()
    for copy in copies:
        copy.wait()


def grads_kernel(
    scalars,
    query,
    output,
    cotangent,
    kv,
    far_values,
    probs,
    zero,
    one,
    two,
    three,
    key_sent,
    key_kept,
    stacked,
    dscores_out,
    keys_out,
    slots,
    keys,
    values,
    parts,
    queries_in,
    output_in,
    gradients_in,
    staged,
    kept,
    done,
):
    fetches = [
        pltpu.make_async_copy(source, target, done.at[index])
        for index, (source, target) in enumerate(
            ((cotangent, gradients_in), (output, output_in), (query, queries_in))
        )
    ]
    stacks = [
        pltpu.make_async_copy(piece.at[1], staged.at[relative], done.at[3 + relative])
        for relative, piece in enumerate((zero, one, two, three))
    ]
    stores = [
        pltpu.make_async_copy(staged.at[relative], stacked.at[relative], done.at[3 + relative])
        for relative in range(4)
    ]
    for copy in fetches + stacks:
        copy.start()
    me = scalars[BLOCKS + NDOC]
    invert_order(scalars, slots)
    parts[...] = jnp.zeros_like(parts)
    for half in range(2):
        _, first = span_of(scalars, half)
        for step in range(SPAN_BLOCKS):
            rows = slice(step * BLOCK, (step + 1) * BLOCK)
            keys[rows, :] = key_block(kv, slots, first, step)
            values[rows, :] = value_block(kv, far_values, slots, first, step, me // 8)
        keys_out[half] = keys[...]
        if half == 0:
            for copy in fetches:
                copy.wait()
        queries, gradients, deltas, shares = [], [], [], []
        for group in range(GROUPS):
            queries.append(heads_of(queries_in, half, group))
            gradients.append(heads_of(gradients_in, half, group))
            forward = heads_of(output_in, half, group).astype(jnp.float32)
            product = gradients[group].astype(jnp.float32) * forward
            deltas.append(jnp.sum(product.T, axis=0, keepdims=True))
            pieces = probs[half * GROUPS + group, SPAN:, :].astype(jnp.float32)
            shares.append(pieces[:1] + pieces[8:9])
        for start, size in chunks():
            rows = slice(start, start + size)
            add = 0.0
            for group in range(GROUPS):
                dprobs = lax.dot_general(
                    values[rows, :],
                    gradients[group],
                    NT,
                    preferred_element_type=jnp.float32,
                )
                weight = probs[half * GROUPS + group, rows, :].astype(jnp.float32) * shares[group]
                dscores = (weight * (dprobs - deltas[group])).astype(jnp.bfloat16)
                add = add + jnp.dot(dscores, queries[group], preferred_element_type=jnp.float32)
                dscores_out[half * GROUPS + group, rows, :] = dscores
            for step in range(size // BLOCK):
                target = slot_rows(slots, first, start // BLOCK + step)
                parts[target, :] += add[step * BLOCK : (step + 1) * BLOCK]
        if half == 0:
            for copy, store in zip(stacks, stores):
                copy.wait()
                store.start()
    keep = pltpu.make_async_copy(kept, key_kept, done.at[7])
    for half, part in enumerate((kept, key_sent)):
        for slot, relative in enumerate((0, 7, 2, 5, 1, 6, 3, 4)):
            start = pl.multiple_of((me ^ (half * 8 + relative)) * ROWS, ROWS)
            part[slot] = (parts[pl.ds(start, ROWS), :] * SCALE).astype(part.dtype)
        if half == 0:
            keep.start()
    for copy in stores + [keep]:
        copy.wait()


def query_kernel(keys, dscores, query_grad, key_turned, staged, done):
    for half in range(2):
        key_turned[...] = keys[half].T
        for group in range(GROUPS):
            turned = jnp.dot(
                key_turned[...], dscores[half * GROUPS + group], preferred_element_type=jnp.float32
            )
            by_row = (turned * SCALE).T.astype(jnp.bfloat16)
            for head in range(GROUP):
                column = (group * GROUP + head) * HEAD_SIZE
                staged[
                    half * BLOCK : (half + 1) * BLOCK, column : column + HEAD_SIZE
                ] = by_row[head * BLOCK : (head + 1) * BLOCK]
    copy = pltpu.make_async_copy(staged, query_grad, done)
    copy.start()
    copy.wait()


def query_product(keys, dscores):
    return pl.pallas_call(
        query_kernel,
        in_specs=[VMEM_SPEC] * 2,
        out_specs=HBM_SPEC,
        out_shape=pltpu.HBM((ROWS, QUERY_HEADS * HEAD_SIZE), jnp.bfloat16),
        scratch_shapes=[
            pltpu.VMEM((HEAD_SIZE, SPAN), jnp.bfloat16),
            pltpu.VMEM((ROWS, QUERY_HEADS * HEAD_SIZE), jnp.bfloat16),
            pltpu.SemaphoreType.DMA,
        ],
        compiler_params=PARAMS,
        name="query_product",
    )(keys, dscores)


def in_vmem(array):
    return pltpu.with_memory_space_constraint(array, pltpu.VMEM)


def in_hbm(array):
    return pltpu.with_memory_space_constraint(array, pltpu.HBM)


VMEM_SPEC = pl.BlockSpec(memory_space=pltpu.VMEM)
HBM_SPEC = pl.BlockSpec(memory_space=pltpu.HBM)
SMEM_SPEC = pl.BlockSpec(memory_space=pltpu.SMEM)
PARAMS = pltpu.CompilerParams(vmem_limit_bytes=VMEM_LIMIT)


def attention_probs(scalars, query, cotangent, kv):
    return pl.pallas_call(
        probs_kernel,
        in_specs=[SMEM_SPEC, HBM_SPEC, HBM_SPEC, VMEM_SPEC],
        out_specs=[VMEM_SPEC, HBM_SPEC],
        out_shape=[
            jax.ShapeDtypeStruct((2 * GROUPS, SPAN + 16, LANES), jnp.bfloat16),
            pltpu.HBM((KEYS, HEAD_SIZE), jnp.bfloat16),
        ],
        scratch_shapes=[
            pltpu.SMEM((BLOCKS,), jnp.int32),
            pltpu.VMEM((SPAN, HEAD_SIZE), jnp.bfloat16),
            pltpu.VMEM((SPAN, HEAD_SIZE), jnp.float32),
            pltpu.VMEM((SPAN, LANES), jnp.float32),
            pltpu.VMEM((KEYS, HEAD_SIZE), jnp.float32),
            pltpu.VMEM((KEYS, HEAD_SIZE), jnp.bfloat16),
            pltpu.VMEM((ROWS, QUERY_HEADS * HEAD_SIZE), jnp.bfloat16),
            pltpu.VMEM((ROWS, QUERY_HEADS * HEAD_SIZE), jnp.bfloat16),
            pltpu.SemaphoreType.DMA((6,)),
        ],
        compiler_params=PARAMS,
        name="probs_and_value_part",
    )(scalars, in_hbm(query), in_hbm(cotangent), kv)


def attention_grads(scalars, query, output, cotangent, kv, far_values, probs, pieces):
    return pl.pallas_call(
        grads_kernel,
        in_specs=[SMEM_SPEC] + [HBM_SPEC] * 3 + [VMEM_SPEC] * 3 + [HBM_SPEC] * 4,
        out_specs=[VMEM_SPEC] + [HBM_SPEC] * 2 + [VMEM_SPEC] * 2,
        out_shape=[
            jax.ShapeDtypeStruct((8, ROWS, HEAD_SIZE), jnp.bfloat16),
            pltpu.HBM((8, ROWS, HEAD_SIZE), jnp.bfloat16),
            pltpu.HBM((4,) + pieces[0].shape[1:], jnp.bfloat16),
            jax.ShapeDtypeStruct((2 * GROUPS, SPAN, LANES), jnp.bfloat16),
            jax.ShapeDtypeStruct((2, SPAN, HEAD_SIZE), jnp.bfloat16),
        ],
        scratch_shapes=[
            pltpu.SMEM((BLOCKS,), jnp.int32),
            pltpu.VMEM((SPAN, HEAD_SIZE), jnp.bfloat16),
            pltpu.VMEM((SPAN, HEAD_SIZE), jnp.bfloat16),
            pltpu.VMEM((KEYS, HEAD_SIZE), jnp.float32),
            pltpu.VMEM((ROWS, QUERY_HEADS * HEAD_SIZE), jnp.bfloat16),
            pltpu.VMEM((ROWS, QUERY_HEADS * HEAD_SIZE), jnp.bfloat16),
            pltpu.VMEM((ROWS, QUERY_HEADS * HEAD_SIZE), jnp.bfloat16),
            pltpu.VMEM((4,) + pieces[0].shape[1:], jnp.bfloat16),
            pltpu.VMEM((8, ROWS, HEAD_SIZE), jnp.bfloat16),
            pltpu.SemaphoreType.DMA((8,)),
        ],
        compiler_params=PARAMS,
        name="key_part",
    )(scalars, *map(in_hbm, (query, output, cotangent)), kv, far_values, probs, *map(in_hbm, pieces))


def load_kernel(zero, one, two, three, partner, sources, done):
    copies = []
    for relative, mine in enumerate((zero, one, two, three)):
        for other, source in enumerate((mine.at[0], partner.at[relative])):
            target = sources.at[relative, pl.ds(other * ROWS, ROWS), :]
            copies.append(pltpu.make_async_copy(source, target, done.at[2 * relative + other]))
    for copy in copies:
        copy.start()
    for copy in copies:
        copy.wait()


def load_inputs(pieces, partner):
    return pl.pallas_call(
        load_kernel,
        in_specs=[HBM_SPEC] * 5,
        out_specs=VMEM_SPEC,
        out_shape=pltpu.VMEM((4, 2 * ROWS, pieces[0].shape[2]), jnp.bfloat16),
        scratch_shapes=[pltpu.SemaphoreType.DMA((8,))],
        compiler_params=PARAMS,
        name="load_inputs",
    )(*map(in_hbm, pieces), in_hbm(partner))


def split_kernel(place, inputs, zero, one, two, three, staged, done):
    x, core = place[0], place[1]
    fetches, stores = [], []
    for relative, part in enumerate((zero, one, two, three)):
        for other in range(2):
            index = 2 * relative + other
            near = (x ^ relative) * 2 + (core ^ other)
            for low in range(2):
                start = pl.multiple_of((low * 8 + near) * WIDTH, WIDTH)
                fetches.append(
                    pltpu.make_async_copy(
                        inputs.at[:, pl.ds(start, WIDTH)],
                        staged.at[index, :, pl.ds(low * WIDTH, WIDTH)],
                        done.at[2 * index + low],
                    )
                )
            stores.append(
                pltpu.make_async_copy(staged.at[index], part.at[other], done.at[2 * index])
            )
    for copy in fetches:
        copy.start()
    for index, store in enumerate(stores):
        fetches[2 * index].wait()
        fetches[2 * index + 1].wait()
        store.start()
    for store in stores:
        store.wait()


def split_inputs(place, inputs):
    return pl.pallas_call(
        split_kernel,
        in_specs=[SMEM_SPEC, HBM_SPEC],
        out_specs=[HBM_SPEC] * 4,
        out_shape=[pltpu.HBM((2, ROWS, 2 * WIDTH), jnp.bfloat16)] * 4,
        scratch_shapes=[
            pltpu.VMEM((8, ROWS, 2 * WIDTH), jnp.bfloat16),
            pltpu.SemaphoreType.DMA((16,)),
        ],
        compiler_params=PARAMS,
        name="split_inputs",
    )(place, in_hbm(inputs))


def fold(kept, received, next_kept, next_sent):
    total = kept[...].astype(jnp.float32) + received[...].astype(jnp.float32)
    count = next_kept.shape[0]
    next_kept[...] = total[:count]
    next_sent[...] = total[count:].astype(jnp.bfloat16)


def halves_of(kept):
    half = (kept.shape[0] // 2,) + kept.shape[1:]
    return [
        jax.ShapeDtypeStruct(half, jnp.float32),
        jax.ShapeDtypeStruct(half, jnp.bfloat16),
    ]


def spread_kernel(
    blocks, kept, received, after, value_grad, spread, next_kept, next_sent, arrived, low, old, done
):
    count = blocks.shape[0]
    fetches = [
        pltpu.make_async_copy(blocks.at[block], arrived.at[block], done.at[block])
        for block in range(count)
    ]
    fetch_old = pltpu.make_async_copy(kept, old, done.at[count])
    for copy in fetches + [fetch_old]:
        copy.start()
    total = 0.0
    for block in range(count):
        fetches[block].wait()
        total = total + arrived[block].astype(jnp.float32)
    low[...] = total.astype(jnp.bfloat16)
    value_grad[...] = low[...]
    stores = [
        pltpu.make_async_copy(low, spread.at[copy], done.at[copy])
        for copy in range(spread.shape[0])
    ]
    for copy in stores:
        copy.start()
    fetch_old.wait()
    fold(old, received, next_kept, next_sent)
    for copy in stores:
        copy.wait()


def sum_and_spread(blocks, count, kept, received, after):
    shape = blocks.shape[1:]
    return pl.pallas_call(
        spread_kernel,
        in_specs=[HBM_SPEC, HBM_SPEC, VMEM_SPEC, HBM_SPEC],
        out_specs=[VMEM_SPEC, HBM_SPEC, VMEM_SPEC, VMEM_SPEC],
        out_shape=[
            jax.ShapeDtypeStruct(shape, jnp.bfloat16),
            pltpu.HBM((count,) + shape, jnp.bfloat16),
        ]
        + halves_of(kept),
        scratch_shapes=[
            pltpu.VMEM(blocks.shape, jnp.bfloat16),
            pltpu.VMEM(shape, jnp.bfloat16),
            pltpu.VMEM(kept.shape, jnp.bfloat16),
            pltpu.SemaphoreType.DMA((blocks.shape[0] + 1,)),
        ],
        compiler_params=PARAMS,
        name="sum_and_spread",
    )(in_hbm(blocks), in_hbm(kept), received, in_hbm(after))


def join_kernel(key, value, joined, both, done):
    copies = []
    for half in range(2):
        both[half, :ROWS] = key[...]
        both[half, ROWS:] = value[half * BLOCK : (half + 1) * BLOCK]
        for copy in range(half * N_CTX // 2, (half + 1) * N_CTX // 2):
            copies.append(pltpu.make_async_copy(both.at[half], joined.at[copy], done.at[copy]))
            copies[-1].start()
    for copy in copies:
        copy.wait()


def join_keys_values(key, value):
    return pl.pallas_call(
        join_kernel,
        in_specs=[VMEM_SPEC] * 2,
        out_specs=HBM_SPEC,
        out_shape=pltpu.HBM((N_CTX, ROWS + BLOCK, HEAD_SIZE), jnp.bfloat16),
        scratch_shapes=[
            pltpu.VMEM((2, ROWS + BLOCK, HEAD_SIZE), jnp.bfloat16),
            pltpu.SemaphoreType.DMA((N_CTX,)),
        ],
        name="join_keys_values",
    )(key, value)


def weight_kernel(place, values, sources, kept, received, weight_part, next_kept, next_sent):
    x, core = place[0], place[1]
    total = 0.0
    for relative in range(4):
        near = (x ^ relative) * 2
        lhs = jnp.concatenate([values[near + core].T, values[near + (1 - core)].T], axis=1)
        total = total + jnp.dot(lhs, sources[relative], preferred_element_type=jnp.float32)
    for block in range(weight_part.shape[0] // HEAD_SIZE):
        columns = pl.ds(block * HEAD_SIZE, HEAD_SIZE)
        weight_part[columns, :] = total[:, block * HEAD_SIZE : (block + 1) * HEAD_SIZE].T.astype(
            jnp.bfloat16
        )
    fold(kept, received, next_kept, next_sent)


def weight_product(place, values, sources, kept, received):
    return pl.pallas_call(
        weight_kernel,
        in_specs=[SMEM_SPEC] + [VMEM_SPEC] * 4,
        out_specs=[VMEM_SPEC] * 3,
        out_shape=[jax.ShapeDtypeStruct((2 * WIDTH, HEAD_SIZE), jnp.bfloat16)] + halves_of(kept),
        compiler_params=PARAMS,
        name="weight_product",
    )(place, values, in_vmem(sources), kept, received)


def exchange(blocks, axes):
    return lax.all_to_all(blocks, axes, 0, 0, tiled=False)


def summed(blocks):
    return jnp.sum(blocks.astype(jnp.float32), axis=0)


def swapped(block, axis, shift):
    count = lax.axis_size(axis)
    return lax.ppermute(block, axis, [(i, i ^ shift) for i in range(count)])


def local(query, key, value, output, output_cotangent, inputs, doc_lengths, block_order):
    scalars = jnp.concatenate(
        [block_order, doc_lengths[0], lax.axis_index(CTX).astype(jnp.int32)[None]]
    )
    place = jnp.stack([lax.axis_index("x"), lax.axis_index("core")]).astype(jnp.int32)
    near_count, far_count = lax.axis_size(NEAR), lax.axis_size(FAR)
    kv = exchange(join_keys_values(key[0], value[0]), CTX)
    far_values = swapped(kv[:, ROWS:], "yhi", 1)

    parts = split_inputs(place, inputs)
    pieces = [parts[0]] + [swapped(parts[r], "x", r) for r in range(1, 4)]
    probs, value_part = attention_probs(scalars, query[0], output_cotangent[0], kv)
    value_blocks = exchange(value_part.reshape(N_CTX, ROWS, HEAD_SIZE), CTX)
    key_sent, key_kept, stacked, dscores, reached = attention_grads(
        scalars, query[0], output[0], output_cotangent[0], kv, far_values, probs, pieces
    )
    query_grad = query_product(reached, dscores)
    partner = swapped(stacked, "core", 1)
    sources = load_inputs(pieces, partner)
    value_grad, spread, key_kept, key_sent = sum_and_spread(
        value_blocks, near_count, key_kept, swapped(key_sent, "yhi", 1), query_grad
    )
    near_values = exchange(spread, NEAR)
    weight_part, key_kept, key_sent = weight_product(
        place, near_values, sources, key_kept, swapped(key_sent, "z", 1)
    )
    weight_blocks = exchange(weight_part.reshape(far_count, -1, HEAD_SIZE), FAR)
    key_sum = key_kept + swapped(key_sent, "z", 2).astype(jnp.float32)
    received = swapped(key_sum[1:].astype(jnp.bfloat16), "z", 7)
    key_grad = (key_sum[:1] + received.astype(jnp.float32)).astype(jnp.bfloat16)
    weight_grad = summed(weight_blocks)
    return query_grad[None], key_grad, value_grad[None], weight_grad


def solution(mesh):
    fine = Mesh(
        mesh.devices.reshape(2, 4, 2, 2, 8), ("ylo", "x", "core", "yhi", "z")
    )
    dp = ("ylo", "x", "core")
    tokens = P(dp, CTX, None)
    flat = P(dp + CTX, None)
    return jax.shard_map(
        local,
        mesh=fine,
        in_specs=(tokens,) * 5 + (flat, P(dp, None), P()),
        out_specs=(tokens, tokens, tokens, flat),
        check_vma=False,
    )
```

```python
import math

import jax
import jax.numpy as jnp
from jax import lax
from jax.experimental import pallas as pl
from jax.experimental.pallas import tpu as pltpu
from jax.sharding import Mesh, PartitionSpec as P

HEAD_SIZE = 128
QUERY_HEADS = 8
BLOCK = 64
BLOCKS = 32
NDOC = 8
ROWS = 128
KEYS = 2048
N_CTX = 16
CHUNK = 256
WIDE_CHUNK = 512
MOST = 1024
SPAN_BLOCKS = MOST // BLOCK + 1
SPAN = SPAN_BLOCKS * BLOCK
GROUP = 4
GROUPS = QUERY_HEADS // GROUP
LANES = GROUP * BLOCK
SCALE = HEAD_SIZE**-0.5
SCALE_LOG2 = SCALE * math.log2(math.e)
MASKED = -1e30
WIDTH = 512
VMEM_LIMIT = 16 * 1024 * 1024
NT = (((1,), (1,)), ((), ()))

CTX = ("yhi", "z")
NEAR = ("x", "core")
FAR = ("ylo", "yhi", "z")


def chunks(most=CHUNK):
    return [(start, min(most, SPAN - start)) for start in range(0, SPAN, most)]


def fold_rows(tile, op):
    return op(tile.reshape(tile.shape[0] // 8, 8, tile.shape[1]), axis=0)


def heads_of(array, half, group):
    rows = slice(half * BLOCK, (half + 1) * BLOCK)
    first = group * GROUP
    return jnp.concatenate(
        [
            array[rows, (first + head) * HEAD_SIZE : (first + head + 1) * HEAD_SIZE]
            for head in range(GROUP)
        ],
        axis=0,
    )


def invert_order(scalars, slots):
    for slot in range(BLOCKS):
        slots[scalars[slot]] = slot


def span_of(scalars, half):
    own = scalars[2 * scalars[BLOCKS + NDOC] + half]
    start, end = jnp.int32(0), jnp.int32(0)
    for doc in range(NDOC):
        end = end + scalars[BLOCKS + doc]
        start = jnp.where(own * BLOCK >= end, end, start)
    return own, start // BLOCK


def slot_of(slots, first, step):
    return slots[jnp.minimum(first + step, BLOCKS - 1)]


def slot_rows(slots, first, step):
    return pl.ds(pl.multiple_of(slot_of(slots, first, step) * BLOCK, BLOCK), BLOCK)


def key_block(kv, slots, first, step):
    slot = slot_of(slots, first, step)
    rows = pl.ds(pl.multiple_of((slot % 2) * BLOCK, BLOCK), BLOCK)
    return kv[slot // 2, rows, :]


def value_block(kv, far_values, slots, first, step, half):
    slot = slot_of(slots, first, step)
    return jnp.where(slot % 2 == half, kv[slot // 2, ROWS:, :], far_values[slot // 2])


def write_bias(scalars, own, first, bias):
    lane = lax.broadcasted_iota(jnp.int32, (1, HEAD_SIZE), 1)
    high = own * BLOCK + lane % BLOCK
    low, end = jnp.zeros_like(high), jnp.int32(0)
    for doc in range(NDOC):
        end = end + scalars[BLOCKS + doc]
        low = jnp.where(high >= end, end, low)
    for start, size in chunks():
        row = lax.broadcasted_iota(jnp.int32, (size, HEAD_SIZE), 0)
        position = first * BLOCK + start + row
        allowed = (position <= high) & (position >= low)
        bias[start : start + size, :] = jnp.where(allowed, 0.0, MASKED)


def probs_kernel(
    scalars,
    query,
    cotangent,
    kv,
    probs,
    value_part,
    slots,
    keys,
    bias,
    scores,
    parts,
    low_parts,
    queries_in,
    gradients_in,
    done,
):
    fetches = [
        pltpu.make_async_copy(query, queries_in, done.at[0]),
        pltpu.make_async_copy(cotangent, gradients_in, done.at[1]),
    ]
    for copy in fetches:
        copy.start()
    invert_order(scalars, slots)
    parts[...] = jnp.zeros_like(parts)
    firsts = []
    for half in range(2):
        own, first = span_of(scalars, half)
        firsts.append(first)
        for step in range(SPAN_BLOCKS):
            rows = slice(step * BLOCK, (step + 1) * BLOCK)
            keys[half, rows, :] = key_block(kv, slots, first, step)
        write_bias(scalars, own, first, bias.at[half])
    fetches[0].wait()
    tiles = 2 * GROUPS
    queries = [heads_of(queries_in, tile // GROUPS, tile % GROUPS) for tile in range(tiles)]
    tops = [jnp.full((8, LANES), MASKED, jnp.float32) for _ in range(tiles)]
    totals = [jnp.zeros((8, LANES), jnp.float32) for _ in range(tiles)]
    scaled = [None] * tiles

    def score(tile, start, size):
        rows = slice(start, start + size)
        half = tile // GROUPS
        raw = lax.dot_general(
            keys[half, rows, :], queries[tile], NT, preferred_element_type=jnp.float32
        )
        add = bias[half, rows, :]
        masked = raw * SCALE_LOG2 + jnp.concatenate([add, add], axis=1)
        scores[tile % 2, rows, :] = masked
        tops[tile] = jnp.maximum(tops[tile], fold_rows(masked, jnp.max))

    def weigh(tile, start, size):
        rows = slice(start, start + size)
        part = jnp.exp2(scores[tile % 2, rows, :] - tops[tile])
        probs[tile, rows, :] = part.astype(jnp.bfloat16)
        totals[tile] = totals[tile] + fold_rows(part, jnp.sum)

    def finish(tile):
        share = 1.0 / jnp.sum(totals[tile], axis=0, keepdims=True)
        by_row = jnp.broadcast_to(share, (HEAD_SIZE, LANES)).T
        full = heads_of(gradients_in, tile // GROUPS, tile % GROUPS).astype(jnp.float32)
        scaled[tile] = (full * by_row).astype(jnp.bfloat16)
        share = jnp.broadcast_to(share, (8, LANES))
        coarse = share.astype(jnp.bfloat16)
        rest = (share - coarse.astype(jnp.float32)).astype(jnp.bfloat16)
        probs[tile, SPAN:, :] = jnp.concatenate([coarse, rest], axis=0)

    def collect(half, start, size):
        rows = slice(start, start + size)
        add = sum(
            jnp.dot(probs[tile, rows, :], scaled[tile], preferred_element_type=jnp.float32)
            for tile in range(half * GROUPS, (half + 1) * GROUPS)
        )
        for step in range(size // BLOCK):
            target = slot_rows(slots, firsts[half], start // BLOCK + step)
            parts[target, :] += add[step * BLOCK : (step + 1) * BLOCK]

    for start, size in chunks():
        score(0, start, size)
    fetches[1].wait()
    for tile in range(tiles):
        tops[tile] = jnp.max(tops[tile], axis=0, keepdims=True)
        for start, size in chunks():
            if tile + 1 < tiles:
                score(tile + 1, start, size)
            weigh(tile, start, size)
            if tile == tiles - 1:
                collect(0, start, size)
        finish(tile)
    for start, size in chunks():
        collect(1, start, size)
    copies = []
    for piece in range(4):
        rows = pl.ds(piece * KEYS // 4, KEYS // 4)
        low_parts[rows, :] = parts[rows, :].astype(jnp.bfloat16)
        copies.append(
            pltpu.make_async_copy(
                low_parts.at[rows, :], value_part.at[rows, :], done.at[2 + piece]
            )
        )
        copies[-1].start()
    for copy in copies:
        copy.wait()


def grads_kernel(
    scalars,
    query,
    output,
    cotangent,
    kv,
    far_values,
    probs,
    zero,
    one,
    two,
    three,
    key_sent,
    key_kept,
    stacked,
    dscores_out,
    keys_out,
    slots,
    values,
    parts,
    queries_in,
    output_in,
    gradients_in,
    staged,
    kept,
    done,
):
    fetches = [
        pltpu.make_async_copy(source, target, done.at[index])
        for index, (source, target) in enumerate(
            ((cotangent, gradients_in), (output, output_in), (query, queries_in))
        )
    ]
    stacks = [
        pltpu.make_async_copy(piece.at[1], staged.at[relative], done.at[3 + relative])
        for relative, piece in enumerate((zero, one, two, three))
    ]
    stores = [
        pltpu.make_async_copy(staged.at[relative], stacked.at[relative], done.at[3 + relative])
        for relative in range(4)
    ]
    for copy in fetches + stacks:
        copy.start()
    me = scalars[BLOCKS + NDOC]
    invert_order(scalars, slots)
    parts[...] = jnp.zeros_like(parts)
    firsts = []
    for half in range(2):
        _, first = span_of(scalars, half)
        firsts.append(first)
        for step in range(SPAN_BLOCKS):
            rows = slice(step * BLOCK, (step + 1) * BLOCK)
            keys_out[half, rows, :] = key_block(kv, slots, first, step)
            values[half, rows, :] = value_block(kv, far_values, slots, first, step, me // 8)
    for copy in fetches:
        copy.wait()
    for half in range(2):
        first = firsts[half]
        queries, gradients, deltas, shares = [], [], [], []
        for group in range(GROUPS):
            queries.append(heads_of(queries_in, half, group))
            gradients.append(heads_of(gradients_in, half, group))
            forward = heads_of(output_in, half, group).astype(jnp.float32)
            product = gradients[group].astype(jnp.float32) * forward
            deltas.append(jnp.sum(product.T, axis=0, keepdims=True))
            pieces = probs[half * GROUPS + group, SPAN:, :].astype(jnp.float32)
            shares.append(pieces[:1] + pieces[8:9])
        for start, size in chunks(WIDE_CHUNK):
            rows = slice(start, start + size)
            add = 0.0
            for group in range(GROUPS):
                dprobs = lax.dot_general(
                    values[half, rows, :],
                    gradients[group],
                    NT,
                    preferred_element_type=jnp.float32,
                )
                weight = probs[half * GROUPS + group, rows, :].astype(jnp.float32) * shares[group]
                dscores = (weight * (dprobs - deltas[group])).astype(jnp.bfloat16)
                add = add + jnp.dot(dscores, queries[group], preferred_element_type=jnp.float32)
                dscores_out[half * GROUPS + group, rows, :] = dscores
            for step in range(size // BLOCK):
                target = slot_rows(slots, first, start // BLOCK + step)
                parts[target, :] += add[step * BLOCK : (step + 1) * BLOCK]
        if half == 0:
            for copy, store in zip(stacks, stores):
                copy.wait()
                store.start()
    keep = pltpu.make_async_copy(kept, key_kept, done.at[7])
    for half, part in enumerate((kept, key_sent)):
        for slot, relative in enumerate((0, 7, 2, 5, 1, 6, 3, 4)):
            start = pl.multiple_of((me ^ (half * 8 + relative)) * ROWS, ROWS)
            part[slot] = (parts[pl.ds(start, ROWS), :] * SCALE).astype(part.dtype)
        if half == 0:
            keep.start()
    for copy in stores + [keep]:
        copy.wait()


def query_kernel(keys, dscores, query_grad, key_turned, staged, done):
    for half in range(2):
        key_turned[...] = keys[half].T
        for group in range(GROUPS):
            turned = jnp.dot(
                key_turned[...], dscores[half * GROUPS + group], preferred_element_type=jnp.float32
            )
            by_row = (turned * SCALE).T.astype(jnp.bfloat16)
            for head in range(GROUP):
                column = (group * GROUP + head) * HEAD_SIZE
                staged[
                    half * BLOCK : (half + 1) * BLOCK, column : column + HEAD_SIZE
                ] = by_row[head * BLOCK : (head + 1) * BLOCK]
    copy = pltpu.make_async_copy(staged, query_grad, done)
    copy.start()
    copy.wait()


def query_product(keys, dscores):
    return pl.pallas_call(
        query_kernel,
        in_specs=[VMEM_SPEC] * 2,
        out_specs=HBM_SPEC,
        out_shape=pltpu.HBM((ROWS, QUERY_HEADS * HEAD_SIZE), jnp.bfloat16),
        scratch_shapes=[
            pltpu.VMEM((HEAD_SIZE, SPAN), jnp.bfloat16),
            pltpu.VMEM((ROWS, QUERY_HEADS * HEAD_SIZE), jnp.bfloat16),
            pltpu.SemaphoreType.DMA,
        ],
        compiler_params=PARAMS,
        name="query_product",
    )(keys, dscores)


def in_vmem(array):
    return pltpu.with_memory_space_constraint(array, pltpu.VMEM)


def in_hbm(array):
    return pltpu.with_memory_space_constraint(array, pltpu.HBM)


VMEM_SPEC = pl.BlockSpec(memory_space=pltpu.VMEM)
HBM_SPEC = pl.BlockSpec(memory_space=pltpu.HBM)
SMEM_SPEC = pl.BlockSpec(memory_space=pltpu.SMEM)
PARAMS = pltpu.CompilerParams(vmem_limit_bytes=VMEM_LIMIT)


def attention_probs(scalars, query, cotangent, kv):
    return pl.pallas_call(
        probs_kernel,
        in_specs=[SMEM_SPEC, HBM_SPEC, HBM_SPEC, VMEM_SPEC],
        out_specs=[VMEM_SPEC, HBM_SPEC],
        out_shape=[
            jax.ShapeDtypeStruct((2 * GROUPS, SPAN + 16, LANES), jnp.bfloat16),
            pltpu.HBM((KEYS, HEAD_SIZE), jnp.bfloat16),
        ],
        scratch_shapes=[
            pltpu.SMEM((BLOCKS,), jnp.int32),
            pltpu.VMEM((2, SPAN, HEAD_SIZE), jnp.bfloat16),
            pltpu.VMEM((2, SPAN, HEAD_SIZE), jnp.float32),
            pltpu.VMEM((2, SPAN, LANES), jnp.float32),
            pltpu.VMEM((KEYS, HEAD_SIZE), jnp.float32),
            pltpu.VMEM((KEYS, HEAD_SIZE), jnp.bfloat16),
            pltpu.VMEM((ROWS, QUERY_HEADS * HEAD_SIZE), jnp.bfloat16),
            pltpu.VMEM((ROWS, QUERY_HEADS * HEAD_SIZE), jnp.bfloat16),
            pltpu.SemaphoreType.DMA((6,)),
        ],
        compiler_params=PARAMS,
        name="probs_and_value_part",
    )(scalars, in_hbm(query), in_hbm(cotangent), kv)


def attention_grads(scalars, query, output, cotangent, kv, far_values, probs, pieces):
    return pl.pallas_call(
        grads_kernel,
        in_specs=[SMEM_SPEC] + [HBM_SPEC] * 3 + [VMEM_SPEC] * 3 + [HBM_SPEC] * 4,
        out_specs=[VMEM_SPEC] + [HBM_SPEC] * 2 + [VMEM_SPEC] * 2,
        out_shape=[
            jax.ShapeDtypeStruct((8, ROWS, HEAD_SIZE), jnp.bfloat16),
            pltpu.HBM((8, ROWS, HEAD_SIZE), jnp.bfloat16),
            pltpu.HBM((4,) + pieces[0].shape[1:], jnp.bfloat16),
            jax.ShapeDtypeStruct((2 * GROUPS, SPAN, LANES), jnp.bfloat16),
            jax.ShapeDtypeStruct((2, SPAN, HEAD_SIZE), jnp.bfloat16),
        ],
        scratch_shapes=[
            pltpu.SMEM((BLOCKS,), jnp.int32),
            pltpu.VMEM((2, SPAN, HEAD_SIZE), jnp.bfloat16),
            pltpu.VMEM((KEYS, HEAD_SIZE), jnp.float32),
            pltpu.VMEM((ROWS, QUERY_HEADS * HEAD_SIZE), jnp.bfloat16),
            pltpu.VMEM((ROWS, QUERY_HEADS * HEAD_SIZE), jnp.bfloat16),
            pltpu.VMEM((ROWS, QUERY_HEADS * HEAD_SIZE), jnp.bfloat16),
            pltpu.VMEM((4,) + pieces[0].shape[1:], jnp.bfloat16),
            pltpu.VMEM((8, ROWS, HEAD_SIZE), jnp.bfloat16),
            pltpu.SemaphoreType.DMA((8,)),
        ],
        compiler_params=PARAMS,
        name="key_part",
    )(scalars, *map(in_hbm, (query, output, cotangent)), kv, far_values, probs, *map(in_hbm, pieces))


def load_kernel(zero, one, two, three, partner, sources, done):
    copies = []
    for relative, mine in enumerate((zero, one, two, three)):
        for other, source in enumerate((mine.at[0], partner.at[relative])):
            target = sources.at[relative, pl.ds(other * ROWS, ROWS), :]
            copies.append(pltpu.make_async_copy(source, target, done.at[2 * relative + other]))
    for copy in copies:
        copy.start()
    for copy in copies:
        copy.wait()


def load_inputs(pieces, partner):
    return pl.pallas_call(
        load_kernel,
        in_specs=[HBM_SPEC] * 5,
        out_specs=VMEM_SPEC,
        out_shape=pltpu.VMEM((4, 2 * ROWS, pieces[0].shape[2]), jnp.bfloat16),
        scratch_shapes=[pltpu.SemaphoreType.DMA((8,))],
        compiler_params=PARAMS,
        name="load_inputs",
    )(*map(in_hbm, pieces), in_hbm(partner))


def split_kernel(place, inputs, zero, one, two, three, staged, done):
    x, core = place[0], place[1]
    fetches, stores = [], []
    for relative, part in enumerate((zero, one, two, three)):
        for other in range(2):
            index = 2 * relative + other
            near = (x ^ relative) * 2 + (core ^ other)
            for low in range(2):
                start = pl.multiple_of((low * 8 + near) * WIDTH, WIDTH)
                fetches.append(
                    pltpu.make_async_copy(
                        inputs.at[:, pl.ds(start, WIDTH)],
                        staged.at[index, :, pl.ds(low * WIDTH, WIDTH)],
                        done.at[2 * index + low],
                    )
                )
            stores.append(
                pltpu.make_async_copy(staged.at[index], part.at[other], done.at[2 * index])
            )
    for copy in fetches:
        copy.start()
    for index, store in enumerate(stores):
        fetches[2 * index].wait()
        fetches[2 * index + 1].wait()
        store.start()
    for store in stores:
        store.wait()


def split_inputs(place, inputs):
    return pl.pallas_call(
        split_kernel,
        in_specs=[SMEM_SPEC, HBM_SPEC],
        out_specs=[HBM_SPEC] * 4,
        out_shape=[pltpu.HBM((2, ROWS, 2 * WIDTH), jnp.bfloat16)] * 4,
        scratch_shapes=[
            pltpu.VMEM((8, ROWS, 2 * WIDTH), jnp.bfloat16),
            pltpu.SemaphoreType.DMA((16,)),
        ],
        compiler_params=PARAMS,
        name="split_inputs",
    )(place, in_hbm(inputs))


def fold(kept, received, next_kept, next_sent):
    total = kept[...].astype(jnp.float32) + received[...].astype(jnp.float32)
    count = next_kept.shape[0]
    next_kept[...] = total[:count]
    next_sent[...] = total[count:].astype(jnp.bfloat16)


def halves_of(kept):
    half = (kept.shape[0] // 2,) + kept.shape[1:]
    return [
        jax.ShapeDtypeStruct(half, jnp.float32),
        jax.ShapeDtypeStruct(half, jnp.bfloat16),
    ]


def spread_kernel(
    blocks, kept, received, after, value_grad, spread, next_kept, next_sent, arrived, low, old, done
):
    count = blocks.shape[0]
    fetches = [
        pltpu.make_async_copy(blocks.at[block], arrived.at[block], done.at[block])
        for block in range(count)
    ]
    fetch_old = pltpu.make_async_copy(kept, old, done.at[count])
    for copy in fetches + [fetch_old]:
        copy.start()
    total = 0.0
    for block in range(count):
        fetches[block].wait()
        total = total + arrived[block].astype(jnp.float32)
    total = total.astype(jnp.bfloat16)
    low[...] = total
    value_grad[...] = total
    stores = [
        pltpu.make_async_copy(low, spread.at[copy], done.at[copy])
        for copy in range(spread.shape[0])
    ]
    for copy in stores:
        copy.start()
    fetch_old.wait()
    fold(old, received, next_kept, next_sent)
    for copy in stores:
        copy.wait()


def sum_and_spread(blocks, count, kept, received, after):
    shape = blocks.shape[1:]
    return pl.pallas_call(
        spread_kernel,
        in_specs=[HBM_SPEC, HBM_SPEC, VMEM_SPEC, HBM_SPEC],
        out_specs=[VMEM_SPEC, HBM_SPEC, VMEM_SPEC, VMEM_SPEC],
        out_shape=[
            jax.ShapeDtypeStruct(shape, jnp.bfloat16),
            pltpu.HBM((count,) + shape, jnp.bfloat16),
        ]
        + halves_of(kept),
        scratch_shapes=[
            pltpu.VMEM(blocks.shape, jnp.bfloat16),
            pltpu.VMEM(shape, jnp.bfloat16),
            pltpu.VMEM(kept.shape, jnp.bfloat16),
            pltpu.SemaphoreType.DMA((blocks.shape[0] + 1,)),
        ],
        compiler_params=PARAMS,
        name="sum_and_spread",
    )(in_hbm(blocks), in_hbm(kept), received, in_hbm(after))


def join_kernel(key, value, joined, both, done):
    copies = []
    for half in range(2):
        both[half, :ROWS] = key[...]
        both[half, ROWS:] = value[half * BLOCK : (half + 1) * BLOCK]
        for copy in range(half * N_CTX // 2, (half + 1) * N_CTX // 2):
            copies.append(pltpu.make_async_copy(both.at[half], joined.at[copy], done.at[copy]))
            copies[-1].start()
    for copy in copies:
        copy.wait()


def join_keys_values(key, value):
    return pl.pallas_call(
        join_kernel,
        in_specs=[VMEM_SPEC] * 2,
        out_specs=HBM_SPEC,
        out_shape=pltpu.HBM((N_CTX, ROWS + BLOCK, HEAD_SIZE), jnp.bfloat16),
        scratch_shapes=[
            pltpu.VMEM((2, ROWS + BLOCK, HEAD_SIZE), jnp.bfloat16),
            pltpu.SemaphoreType.DMA((N_CTX,)),
        ],
        name="join_keys_values",
    )(key, value)


def weight_kernel(place, values, sources, kept, received, weight_part, next_kept, next_sent):
    x, core = place[0], place[1]
    total = 0.0
    for relative in range(4):
        near = (x ^ relative) * 2
        lhs = jnp.concatenate([values[near + core].T, values[near + (1 - core)].T], axis=1)
        total = total + jnp.dot(lhs, sources[relative], preferred_element_type=jnp.float32)
    for block in range(weight_part.shape[0] // HEAD_SIZE):
        columns = pl.ds(block * HEAD_SIZE, HEAD_SIZE)
        weight_part[columns, :] = total[:, block * HEAD_SIZE : (block + 1) * HEAD_SIZE].T.astype(
            jnp.bfloat16
        )
    fold(kept, received, next_kept, next_sent)


def weight_product(place, values, sources, kept, received):
    return pl.pallas_call(
        weight_kernel,
        in_specs=[SMEM_SPEC] + [VMEM_SPEC] * 4,
        out_specs=[VMEM_SPEC] * 3,
        out_shape=[jax.ShapeDtypeStruct((2 * WIDTH, HEAD_SIZE), jnp.bfloat16)] + halves_of(kept),
        compiler_params=PARAMS,
        name="weight_product",
    )(place, values, in_vmem(sources), kept, received)


def exchange(blocks, axes):
    return lax.all_to_all(blocks, axes, 0, 0, tiled=False)


def summed(blocks):
    return jnp.sum(blocks.astype(jnp.float32), axis=0)


def swapped(block, axis, shift):
    count = lax.axis_size(axis)
    return lax.ppermute(block, axis, [(i, i ^ shift) for i in range(count)])


def local(query, key, value, output, output_cotangent, inputs, doc_lengths, block_order):
    scalars = jnp.concatenate(
        [block_order, doc_lengths[0], lax.axis_index(CTX).astype(jnp.int32)[None]]
    )
    place = jnp.stack([lax.axis_index("x"), lax.axis_index("core")]).astype(jnp.int32)
    near_count, far_count = lax.axis_size(NEAR), lax.axis_size(FAR)
    kv = exchange(join_keys_values(key[0], value[0]), CTX)
    far_values = swapped(kv[:, ROWS:], "yhi", 1)

    parts = split_inputs(place, inputs)
    pieces = [parts[0]] + [swapped(parts[r], "x", r) for r in range(1, 4)]
    probs, value_part = attention_probs(scalars, query[0], output_cotangent[0], kv)
    value_blocks = exchange(value_part.reshape(N_CTX, ROWS, HEAD_SIZE), CTX)
    key_sent, key_kept, stacked, dscores, reached = attention_grads(
        scalars, query[0], output[0], output_cotangent[0], kv, far_values, probs, pieces
    )
    query_grad = query_product(reached, dscores)
    partner = swapped(stacked, "core", 1)
    sources = load_inputs(pieces, partner)
    value_grad, spread, key_kept, key_sent = sum_and_spread(
        value_blocks, near_count, key_kept, swapped(key_sent, "yhi", 1), query_grad
    )
    near_values = exchange(spread, NEAR)
    weight_part, key_kept, key_sent = weight_product(
        place, near_values, sources, key_kept, swapped(key_sent, "z", 1)
    )
    weight_blocks = exchange(weight_part.reshape(far_count, -1, HEAD_SIZE), FAR)
    key_sum = key_kept + swapped(key_sent, "z", 2).astype(jnp.float32)
    received = swapped(key_sum[1:].astype(jnp.bfloat16), "z", 7)
    key_grad = (key_sum[:1] + received.astype(jnp.float32)).astype(jnp.bfloat16)
    weight_grad = summed(weight_blocks)
    return query_grad[None], key_grad, value_grad[None], weight_grad


def solution(mesh):
    fine = Mesh(
        mesh.devices.reshape(2, 4, 2, 2, 8), ("ylo", "x", "core", "yhi", "z")
    )
    dp = ("ylo", "x", "core")
    tokens = P(dp, CTX, None)
    flat = P(dp + CTX, None)
    return jax.shard_map(
        local,
        mesh=fine,
        in_specs=(tokens,) * 5 + (flat, P(dp, None), P()),
        out_specs=(tokens, tokens, tokens, flat),
        check_vma=False,
    )
```

```python
import math

import jax
import jax.numpy as jnp
from jax import lax
from jax.experimental import pallas as pl
from jax.experimental.pallas import tpu as pltpu
from jax.sharding import Mesh, PartitionSpec as P

HEAD_SIZE = 128
QUERY_HEADS = 8
BLOCK = 64
BLOCKS = 32
NDOC = 8
ROWS = 128
KEYS = 2048
N_CTX = 16
CHUNK = 256
WIDE_CHUNK = 512
MOST = 1024
SPAN_BLOCKS = MOST // BLOCK + 1
SPAN = SPAN_BLOCKS * BLOCK
GROUP = 4
GROUPS = QUERY_HEADS // GROUP
LANES = GROUP * BLOCK
SCALE = HEAD_SIZE**-0.5
SCALE_LOG2 = SCALE * math.log2(math.e)
MASKED = -1e30
WIDTH = 512
VMEM_LIMIT = 16 * 1024 * 1024
NT = (((1,), (1,)), ((), ()))

CTX = ("yhi", "z")
NEAR = ("x", "core")
FAR = ("ylo", "yhi", "z")


def chunks(most=CHUNK):
    return [(start, min(most, SPAN - start)) for start in range(0, SPAN, most)]


def fold_rows(tile, op):
    return op(tile.reshape(tile.shape[0] // 8, 8, tile.shape[1]), axis=0)


def heads_of(array, half, group):
    rows = slice(half * BLOCK, (half + 1) * BLOCK)
    first = group * GROUP
    return jnp.concatenate(
        [
            array[rows, (first + head) * HEAD_SIZE : (first + head + 1) * HEAD_SIZE]
            for head in range(GROUP)
        ],
        axis=0,
    )


def invert_order(scalars, slots):
    for slot in range(BLOCKS):
        slots[scalars[slot]] = slot


def span_of(scalars, half):
    own = scalars[2 * scalars[BLOCKS + NDOC] + half]
    start, end = jnp.int32(0), jnp.int32(0)
    for doc in range(NDOC):
        end = end + scalars[BLOCKS + doc]
        start = jnp.where(own * BLOCK >= end, end, start)
    return own, start // BLOCK


def slot_of(slots, first, step):
    return slots[jnp.minimum(first + step, BLOCKS - 1)]


def slot_rows(slots, first, step):
    return pl.ds(pl.multiple_of(slot_of(slots, first, step) * BLOCK, BLOCK), BLOCK)


def key_block(kv, slots, first, step):
    slot = slot_of(slots, first, step)
    rows = pl.ds(pl.multiple_of((slot % 2) * BLOCK, BLOCK), BLOCK)
    return kv[slot // 2, rows, :]


def value_block(kv, far_values, slots, first, step, half):
    slot = slot_of(slots, first, step)
    return jnp.where(slot % 2 == half, kv[slot // 2, ROWS:, :], far_values[slot // 2])


def write_bias(scalars, own, first, bias):
    lane = lax.broadcasted_iota(jnp.int32, (1, HEAD_SIZE), 1)
    high = own * BLOCK + lane % BLOCK
    low, end = jnp.zeros_like(high), jnp.int32(0)
    for doc in range(NDOC):
        end = end + scalars[BLOCKS + doc]
        low = jnp.where(high >= end, end, low)
    for start, size in chunks():
        row = lax.broadcasted_iota(jnp.int32, (size, HEAD_SIZE), 0)
        position = first * BLOCK + start + row
        allowed = (position <= high) & (position >= low)
        bias[start : start + size, :] = jnp.where(allowed, 0.0, MASKED)


def probs_kernel(
    scalars,
    query,
    cotangent,
    kv,
    probs,
    value_part,
    far_sent,
    slots,
    keys,
    bias,
    scores,
    parts,
    low_parts,
    queries_in,
    gradients_in,
    done,
):
    fetches = [
        pltpu.make_async_copy(query, queries_in, done.at[0]),
        pltpu.make_async_copy(cotangent, gradients_in, done.at[1]),
    ]
    far = pltpu.make_async_copy(kv.at[:, pl.ds(ROWS, BLOCK), :], far_sent, done.at[6])
    for copy in fetches + [far]:
        copy.start()
    invert_order(scalars, slots)
    parts[...] = jnp.zeros_like(parts)
    firsts = []
    for half in range(2):
        own, first = span_of(scalars, half)
        firsts.append(first)
        for step in range(SPAN_BLOCKS):
            rows = slice(step * BLOCK, (step + 1) * BLOCK)
            keys[half, rows, :] = key_block(kv, slots, first, step)
        write_bias(scalars, own, first, bias.at[half])
    fetches[0].wait()
    tiles = 2 * GROUPS
    queries = [heads_of(queries_in, tile // GROUPS, tile % GROUPS) for tile in range(tiles)]
    tops = [jnp.full((8, LANES), MASKED, jnp.float32) for _ in range(tiles)]
    totals = [jnp.zeros((8, LANES), jnp.float32) for _ in range(tiles)]
    scaled = [None] * tiles

    def score(tile, start, size):
        rows = slice(start, start + size)
        half = tile // GROUPS
        raw = lax.dot_general(
            keys[half, rows, :], queries[tile], NT, preferred_element_type=jnp.float32
        )
        add = bias[half, rows, :]
        masked = raw * SCALE_LOG2 + jnp.concatenate([add, add], axis=1)
        scores[tile % 2, rows, :] = masked
        tops[tile] = jnp.maximum(tops[tile], fold_rows(masked, jnp.max))

    def weigh(tile, start, size):
        rows = slice(start, start + size)
        part = jnp.exp2(scores[tile % 2, rows, :] - tops[tile])
        probs[tile, rows, :] = part.astype(jnp.bfloat16)
        totals[tile] = totals[tile] + fold_rows(part, jnp.sum)

    def finish(tile):
        share = 1.0 / jnp.sum(totals[tile], axis=0, keepdims=True)
        by_row = jnp.broadcast_to(share, (HEAD_SIZE, LANES)).T
        full = heads_of(gradients_in, tile // GROUPS, tile % GROUPS).astype(jnp.float32)
        scaled[tile] = (full * by_row).astype(jnp.bfloat16)
        share = jnp.broadcast_to(share, (8, LANES))
        coarse = share.astype(jnp.bfloat16)
        rest = (share - coarse.astype(jnp.float32)).astype(jnp.bfloat16)
        probs[tile, SPAN:, :] = jnp.concatenate([coarse, rest], axis=0)

    def collect(half, start, size):
        rows = slice(start, start + size)
        add = sum(
            jnp.dot(probs[tile, rows, :], scaled[tile], preferred_element_type=jnp.float32)
            for tile in range(half * GROUPS, (half + 1) * GROUPS)
        )
        for step in range(size // BLOCK):
            target = slot_rows(slots, firsts[half], start // BLOCK + step)
            parts[target, :] += add[step * BLOCK : (step + 1) * BLOCK]

    for start, size in chunks():
        score(0, start, size)
    fetches[1].wait()
    for tile in range(tiles):
        tops[tile] = jnp.max(tops[tile], axis=0, keepdims=True)
        for start, size in chunks():
            if tile + 1 < tiles:
                score(tile + 1, start, size)
            weigh(tile, start, size)
            if tile == tiles - 1:
                collect(0, start, size)
        finish(tile)
    for start, size in chunks():
        collect(1, start, size)
    copies = []
    for piece in range(4):
        rows = pl.ds(piece * KEYS // 4, KEYS // 4)
        low_parts[rows, :] = parts[rows, :].astype(jnp.bfloat16)
        copies.append(
            pltpu.make_async_copy(
                low_parts.at[rows, :], value_part.at[rows, :], done.at[2 + piece]
            )
        )
        copies[-1].start()
    for copy in copies + [far]:
        copy.wait()


def grads_kernel(
    scalars,
    query,
    output,
    cotangent,
    kv,
    far_values,
    probs,
    zero,
    one,
    two,
    three,
    key_sent,
    key_kept,
    stacked,
    dscores_out,
    keys_out,
    slots,
    values,
    parts,
    queries_in,
    output_in,
    gradients_in,
    staged,
    kept,
    done,
):
    fetches = [
        pltpu.make_async_copy(source, target, done.at[index])
        for index, (source, target) in enumerate(
            ((cotangent, gradients_in), (output, output_in), (query, queries_in))
        )
    ]
    stacks = [
        pltpu.make_async_copy(piece.at[1], staged.at[relative], done.at[3 + relative])
        for relative, piece in enumerate((zero, one, two, three))
    ]
    stores = [
        pltpu.make_async_copy(staged.at[relative], stacked.at[relative], done.at[3 + relative])
        for relative in range(4)
    ]
    for copy in fetches + stacks:
        copy.start()
    me = scalars[BLOCKS + NDOC]
    invert_order(scalars, slots)
    parts[...] = jnp.zeros_like(parts)
    firsts = []
    for half in range(2):
        _, first = span_of(scalars, half)
        firsts.append(first)
        for step in range(SPAN_BLOCKS):
            rows = slice(step * BLOCK, (step + 1) * BLOCK)
            keys_out[half, rows, :] = key_block(kv, slots, first, step)
            values[half, rows, :] = value_block(kv, far_values, slots, first, step, me // 8)
    for copy in fetches:
        copy.wait()
    for half in range(2):
        first = firsts[half]
        queries, gradients, deltas, shares = [], [], [], []
        for group in range(GROUPS):
            queries.append(heads_of(queries_in, half, group))
            gradients.append(heads_of(gradients_in, half, group))
            forward = heads_of(output_in, half, group).astype(jnp.float32)
            product = gradients[group].astype(jnp.float32) * forward
            deltas.append(jnp.sum(product.T, axis=0, keepdims=True))
            pieces = probs[half * GROUPS + group, SPAN:, :].astype(jnp.float32)
            shares.append(pieces[:1] + pieces[8:9])
        for start, size in chunks(WIDE_CHUNK):
            rows = slice(start, start + size)
            add = 0.0
            for group in range(GROUPS):
                dprobs = lax.dot_general(
                    values[half, rows, :],
                    gradients[group],
                    NT,
                    preferred_element_type=jnp.float32,
                )
                weight = probs[half * GROUPS + group, rows, :].astype(jnp.float32) * shares[group]
                dscores = (weight * (dprobs - deltas[group])).astype(jnp.bfloat16)
                add = add + jnp.dot(dscores, queries[group], preferred_element_type=jnp.float32)
                dscores_out[half * GROUPS + group, rows, :] = dscores
            for step in range(size // BLOCK):
                target = slot_rows(slots, first, start // BLOCK + step)
                parts[target, :] += add[step * BLOCK : (step + 1) * BLOCK]
        if half == 0:
            for copy, store in zip(stacks, stores):
                copy.wait()
                store.start()
    keep = pltpu.make_async_copy(kept, key_kept, done.at[7])
    for half, part in enumerate((kept, key_sent)):
        for slot, relative in enumerate((0, 7, 2, 5, 1, 6, 3, 4)):
            start = pl.multiple_of((me ^ (half * 8 + relative)) * ROWS, ROWS)
            part[slot] = (parts[pl.ds(start, ROWS), :] * SCALE).astype(part.dtype)
        if half == 0:
            keep.start()
    for copy in stores + [keep]:
        copy.wait()


def query_kernel(keys, dscores, query_grad, key_turned, staged, done):
    for half in range(2):
        key_turned[...] = keys[half].T
        for group in range(GROUPS):
            turned = jnp.dot(
                key_turned[...], dscores[half * GROUPS + group], preferred_element_type=jnp.float32
            )
            by_row = (turned * SCALE).T.astype(jnp.bfloat16)
            for head in range(GROUP):
                column = (group * GROUP + head) * HEAD_SIZE
                staged[
                    half * BLOCK : (half + 1) * BLOCK, column : column + HEAD_SIZE
                ] = by_row[head * BLOCK : (head + 1) * BLOCK]
    copy = pltpu.make_async_copy(staged, query_grad, done)
    copy.start()
    copy.wait()


def query_product(keys, dscores):
    return pl.pallas_call(
        query_kernel,
        in_specs=[VMEM_SPEC] * 2,
        out_specs=HBM_SPEC,
        out_shape=pltpu.HBM((ROWS, QUERY_HEADS * HEAD_SIZE), jnp.bfloat16),
        scratch_shapes=[
            pltpu.VMEM((HEAD_SIZE, SPAN), jnp.bfloat16),
            pltpu.VMEM((ROWS, QUERY_HEADS * HEAD_SIZE), jnp.bfloat16),
            pltpu.SemaphoreType.DMA,
        ],
        compiler_params=PARAMS,
        name="query_product",
    )(keys, dscores)


def in_vmem(array):
    return pltpu.with_memory_space_constraint(array, pltpu.VMEM)


def in_hbm(array):
    return pltpu.with_memory_space_constraint(array, pltpu.HBM)


VMEM_SPEC = pl.BlockSpec(memory_space=pltpu.VMEM)
HBM_SPEC = pl.BlockSpec(memory_space=pltpu.HBM)
SMEM_SPEC = pl.BlockSpec(memory_space=pltpu.SMEM)
PARAMS = pltpu.CompilerParams(vmem_limit_bytes=VMEM_LIMIT)


def attention_probs(scalars, query, cotangent, kv):
    return pl.pallas_call(
        probs_kernel,
        in_specs=[SMEM_SPEC, HBM_SPEC, HBM_SPEC, VMEM_SPEC],
        out_specs=[VMEM_SPEC, HBM_SPEC, HBM_SPEC],
        out_shape=[
            jax.ShapeDtypeStruct((2 * GROUPS, SPAN + 16, LANES), jnp.bfloat16),
            pltpu.HBM((KEYS, HEAD_SIZE), jnp.bfloat16),
            pltpu.HBM((N_CTX, BLOCK, HEAD_SIZE), jnp.bfloat16),
        ],
        scratch_shapes=[
            pltpu.SMEM((BLOCKS,), jnp.int32),
            pltpu.VMEM((2, SPAN, HEAD_SIZE), jnp.bfloat16),
            pltpu.VMEM((2, SPAN, HEAD_SIZE), jnp.float32),
            pltpu.VMEM((2, SPAN, LANES), jnp.float32),
            pltpu.VMEM((KEYS, HEAD_SIZE), jnp.float32),
            pltpu.VMEM((KEYS, HEAD_SIZE), jnp.bfloat16),
            pltpu.VMEM((ROWS, QUERY_HEADS * HEAD_SIZE), jnp.bfloat16),
            pltpu.VMEM((ROWS, QUERY_HEADS * HEAD_SIZE), jnp.bfloat16),
            pltpu.SemaphoreType.DMA((7,)),
        ],
        compiler_params=PARAMS,
        name="probs_and_value_part",
    )(scalars, in_hbm(query), in_hbm(cotangent), kv)


def attention_grads(scalars, query, output, cotangent, kv, far_values, probs, pieces):
    return pl.pallas_call(
        grads_kernel,
        in_specs=[SMEM_SPEC] + [HBM_SPEC] * 3 + [VMEM_SPEC] * 3 + [HBM_SPEC] * 4,
        out_specs=[VMEM_SPEC] + [HBM_SPEC] * 2 + [VMEM_SPEC] * 2,
        out_shape=[
            jax.ShapeDtypeStruct((8, ROWS, HEAD_SIZE), jnp.bfloat16),
            pltpu.HBM((8, ROWS, HEAD_SIZE), jnp.bfloat16),
            pltpu.HBM((4,) + pieces[0].shape[1:], jnp.bfloat16),
            jax.ShapeDtypeStruct((2 * GROUPS, SPAN, LANES), jnp.bfloat16),
            jax.ShapeDtypeStruct((2, SPAN, HEAD_SIZE), jnp.bfloat16),
        ],
        scratch_shapes=[
            pltpu.SMEM((BLOCKS,), jnp.int32),
            pltpu.VMEM((2, SPAN, HEAD_SIZE), jnp.bfloat16),
            pltpu.VMEM((KEYS, HEAD_SIZE), jnp.float32),
            pltpu.VMEM((ROWS, QUERY_HEADS * HEAD_SIZE), jnp.bfloat16),
            pltpu.VMEM((ROWS, QUERY_HEADS * HEAD_SIZE), jnp.bfloat16),
            pltpu.VMEM((ROWS, QUERY_HEADS * HEAD_SIZE), jnp.bfloat16),
            pltpu.VMEM((4,) + pieces[0].shape[1:], jnp.bfloat16),
            pltpu.VMEM((8, ROWS, HEAD_SIZE), jnp.bfloat16),
            pltpu.SemaphoreType.DMA((8,)),
        ],
        compiler_params=PARAMS,
        name="key_part",
    )(scalars, *map(in_hbm, (query, output, cotangent)), kv, far_values, probs, *map(in_hbm, pieces))


def load_kernel(zero, one, two, three, partner, sources, done):
    copies = []
    for relative, mine in enumerate((zero, one, two, three)):
        for other, source in enumerate((mine.at[0], partner.at[relative])):
            target = sources.at[relative, pl.ds(other * ROWS, ROWS), :]
            copies.append(pltpu.make_async_copy(source, target, done.at[2 * relative + other]))
    for copy in copies:
        copy.start()
    for copy in copies:
        copy.wait()


def load_inputs(pieces, partner):
    return pl.pallas_call(
        load_kernel,
        in_specs=[HBM_SPEC] * 5,
        out_specs=VMEM_SPEC,
        out_shape=pltpu.VMEM((4, 2 * ROWS, pieces[0].shape[2]), jnp.bfloat16),
        scratch_shapes=[pltpu.SemaphoreType.DMA((8,))],
        compiler_params=PARAMS,
        name="load_inputs",
    )(*map(in_hbm, pieces), in_hbm(partner))


def split_kernel(place, inputs, zero, one, two, three, staged, done):
    x, core = place[0], place[1]
    fetches, stores = [], []
    for relative, part in enumerate((zero, one, two, three)):
        for other in range(2):
            index = 2 * relative + other
            near = (x ^ relative) * 2 + (core ^ other)
            for low in range(2):
                start = pl.multiple_of((low * 8 + near) * WIDTH, WIDTH)
                fetches.append(
                    pltpu.make_async_copy(
                        inputs.at[:, pl.ds(start, WIDTH)],
                        staged.at[index, :, pl.ds(low * WIDTH, WIDTH)],
                        done.at[2 * index + low],
                    )
                )
            stores.append(
                pltpu.make_async_copy(staged.at[index], part.at[other], done.at[2 * index])
            )
    for copy in fetches:
        copy.start()
    for index, store in enumerate(stores):
        fetches[2 * index].wait()
        fetches[2 * index + 1].wait()
        store.start()
    for store in stores:
        store.wait()


def split_inputs(place, inputs):
    return pl.pallas_call(
        split_kernel,
        in_specs=[SMEM_SPEC, HBM_SPEC],
        out_specs=[HBM_SPEC] * 4,
        out_shape=[pltpu.HBM((2, ROWS, 2 * WIDTH), jnp.bfloat16)] * 4,
        scratch_shapes=[
            pltpu.VMEM((8, ROWS, 2 * WIDTH), jnp.bfloat16),
            pltpu.SemaphoreType.DMA((16,)),
        ],
        compiler_params=PARAMS,
        name="split_inputs",
    )(place, in_hbm(inputs))


def fold(kept, received, next_kept, next_sent):
    total = kept[...].astype(jnp.float32) + received[...].astype(jnp.float32)
    count = next_kept.shape[0]
    next_kept[...] = total[:count]
    next_sent[...] = total[count:].astype(jnp.bfloat16)


def halves_of(kept):
    half = (kept.shape[0] // 2,) + kept.shape[1:]
    return [
        jax.ShapeDtypeStruct(half, jnp.float32),
        jax.ShapeDtypeStruct(half, jnp.bfloat16),
    ]


def spread_kernel(
    blocks, kept, received, after, value_grad, spread, next_kept, next_sent, arrived, low, old, done
):
    count = blocks.shape[0]
    fetches = [
        pltpu.make_async_copy(blocks.at[block], arrived.at[block], done.at[block])
        for block in range(count)
    ]
    fetch_old = pltpu.make_async_copy(kept, old, done.at[count])
    for copy in fetches + [fetch_old]:
        copy.start()
    total = 0.0
    for block in range(count):
        fetches[block].wait()
        total = total + arrived[block].astype(jnp.float32)
    total = total.astype(jnp.bfloat16)
    low[...] = total
    value_grad[...] = total
    stores = [
        pltpu.make_async_copy(low, spread.at[copy], done.at[copy])
        for copy in range(spread.shape[0])
    ]
    for copy in stores:
        copy.start()
    fetch_old.wait()
    fold(old, received, next_kept, next_sent)
    for copy in stores:
        copy.wait()


def sum_and_spread(blocks, count, kept, received, after):
    shape = blocks.shape[1:]
    return pl.pallas_call(
        spread_kernel,
        in_specs=[HBM_SPEC, HBM_SPEC, VMEM_SPEC, HBM_SPEC],
        out_specs=[VMEM_SPEC, HBM_SPEC, VMEM_SPEC, VMEM_SPEC],
        out_shape=[
            jax.ShapeDtypeStruct(shape, jnp.bfloat16),
            pltpu.HBM((count,) + shape, jnp.bfloat16),
        ]
        + halves_of(kept),
        scratch_shapes=[
            pltpu.VMEM(blocks.shape, jnp.bfloat16),
            pltpu.VMEM(shape, jnp.bfloat16),
            pltpu.VMEM(kept.shape, jnp.bfloat16),
            pltpu.SemaphoreType.DMA((blocks.shape[0] + 1,)),
        ],
        compiler_params=PARAMS,
        name="sum_and_spread",
    )(in_hbm(blocks), in_hbm(kept), received, in_hbm(after))


def join_kernel(key, value, joined, both, done):
    copies = []
    for half in range(2):
        both[half, :ROWS] = key[...]
        both[half, ROWS:] = value[half * BLOCK : (half + 1) * BLOCK]
        for copy in range(half * N_CTX // 2, (half + 1) * N_CTX // 2):
            copies.append(pltpu.make_async_copy(both.at[half], joined.at[copy], done.at[copy]))
            copies[-1].start()
    for copy in copies:
        copy.wait()


def join_keys_values(key, value):
    return pl.pallas_call(
        join_kernel,
        in_specs=[VMEM_SPEC] * 2,
        out_specs=HBM_SPEC,
        out_shape=pltpu.HBM((N_CTX, ROWS + BLOCK, HEAD_SIZE), jnp.bfloat16),
        scratch_shapes=[
            pltpu.VMEM((2, ROWS + BLOCK, HEAD_SIZE), jnp.bfloat16),
            pltpu.SemaphoreType.DMA((N_CTX,)),
        ],
        name="join_keys_values",
    )(key, value)


def weight_kernel(place, values, sources, kept, received, weight_part, next_kept, next_sent):
    x, core = place[0], place[1]
    total = 0.0
    for relative in range(4):
        near = (x ^ relative) * 2
        lhs = jnp.concatenate([values[near + core].T, values[near + (1 - core)].T], axis=1)
        total = total + jnp.dot(lhs, sources[relative], preferred_element_type=jnp.float32)
    for block in range(weight_part.shape[0] // HEAD_SIZE):
        columns = pl.ds(block * HEAD_SIZE, HEAD_SIZE)
        weight_part[columns, :] = total[:, block * HEAD_SIZE : (block + 1) * HEAD_SIZE].T.astype(
            jnp.bfloat16
        )
    fold(kept, received, next_kept, next_sent)


def weight_product(place, values, sources, kept, received):
    return pl.pallas_call(
        weight_kernel,
        in_specs=[SMEM_SPEC] + [VMEM_SPEC] * 4,
        out_specs=[VMEM_SPEC] * 3,
        out_shape=[jax.ShapeDtypeStruct((2 * WIDTH, HEAD_SIZE), jnp.bfloat16)] + halves_of(kept),
        compiler_params=PARAMS,
        name="weight_product",
    )(place, values, in_vmem(sources), kept, received)


def exchange(blocks, axes):
    return lax.all_to_all(blocks, axes, 0, 0, tiled=False)


def summed(blocks):
    return jnp.sum(blocks.astype(jnp.float32), axis=0)


def swapped(block, axis, shift):
    count = lax.axis_size(axis)
    return lax.ppermute(block, axis, [(i, i ^ shift) for i in range(count)])


def local(query, key, value, output, output_cotangent, inputs, doc_lengths, block_order):
    scalars = jnp.concatenate(
        [block_order, doc_lengths[0], lax.axis_index(CTX).astype(jnp.int32)[None]]
    )
    place = jnp.stack([lax.axis_index("x"), lax.axis_index("core")]).astype(jnp.int32)
    near_count, far_count = lax.axis_size(NEAR), lax.axis_size(FAR)
    kv = exchange(join_keys_values(key[0], value[0]), CTX)

    parts = split_inputs(place, inputs)
    pieces = [parts[0]] + [swapped(parts[r], "x", r) for r in range(1, 4)]
    probs, value_part, far_sent = attention_probs(scalars, query[0], output_cotangent[0], kv)
    far_values = swapped(far_sent, "yhi", 1)
    value_blocks = exchange(value_part.reshape(N_CTX, ROWS, HEAD_SIZE), CTX)
    key_sent, key_kept, stacked, dscores, reached = attention_grads(
        scalars, query[0], output[0], output_cotangent[0], kv, far_values, probs, pieces
    )
    query_grad = query_product(reached, dscores)
    partner = swapped(stacked, "core", 1)
    sources = load_inputs(pieces, partner)
    value_grad, spread, key_kept, key_sent = sum_and_spread(
        value_blocks, near_count, key_kept, swapped(key_sent, "yhi", 1), query_grad
    )
    near_values = exchange(spread, NEAR)
    weight_part, key_kept, key_sent = weight_product(
        place, near_values, sources, key_kept, swapped(key_sent, "z", 1)
    )
    weight_blocks = exchange(weight_part.reshape(far_count, -1, HEAD_SIZE), FAR)
    key_sum = key_kept + swapped(key_sent, "z", 2).astype(jnp.float32)
    received = swapped(key_sum[1:].astype(jnp.bfloat16), "z", 7)
    key_grad = (key_sum[:1] + received.astype(jnp.float32)).astype(jnp.bfloat16)
    weight_grad = summed(weight_blocks)
    return query_grad[None], key_grad, value_grad[None], weight_grad


def solution(mesh):
    fine = Mesh(
        mesh.devices.reshape(2, 4, 2, 2, 8), ("ylo", "x", "core", "yhi", "z")
    )
    dp = ("ylo", "x", "core")
    tokens = P(dp, CTX, None)
    flat = P(dp + CTX, None)
    return jax.shard_map(
        local,
        mesh=fine,
        in_specs=(tokens,) * 5 + (flat, P(dp, None), P()),
        out_specs=(tokens, tokens, tokens, flat),
        check_vma=False,
    )
```

```python
import math

import jax
import jax.numpy as jnp
from jax import lax
from jax.experimental import pallas as pl
from jax.experimental.pallas import tpu as pltpu
from jax.sharding import Mesh, PartitionSpec as P

HEAD_SIZE = 128
QUERY_HEADS = 8
BLOCK = 64
BLOCKS = 32
NDOC = 8
ROWS = 128
KEYS = 2048
N_CTX = 16
CHUNK = 256
WIDE_CHUNK = 512
MOST = 1024
SPAN_BLOCKS = MOST // BLOCK + 1
SPAN = SPAN_BLOCKS * BLOCK
GROUP = 4
GROUPS = QUERY_HEADS // GROUP
LANES = GROUP * BLOCK
SCALE = HEAD_SIZE**-0.5
SCALE_LOG2 = SCALE * math.log2(math.e)
MASKED = -1e30
WIDTH = 512
VMEM_LIMIT = 16 * 1024 * 1024
NT = (((1,), (1,)), ((), ()))

CTX = ("yhi", "z")
NEAR = ("x", "core")
FAR = ("ylo", "yhi", "z")


def chunks(most=CHUNK):
    return [(start, min(most, SPAN - start)) for start in range(0, SPAN, most)]


def fold_rows(tile, op):
    return op(tile.reshape(tile.shape[0] // 8, 8, tile.shape[1]), axis=0)


def heads_of(array, half, group):
    rows = slice(half * BLOCK, (half + 1) * BLOCK)
    first = group * GROUP
    return jnp.concatenate(
        [
            array[rows, (first + head) * HEAD_SIZE : (first + head + 1) * HEAD_SIZE]
            for head in range(GROUP)
        ],
        axis=0,
    )


def invert_order(scalars, slots):
    for slot in range(BLOCKS):
        slots[scalars[slot]] = slot


def span_of(scalars, half):
    own = scalars[2 * scalars[BLOCKS + NDOC] + half]
    start, end = jnp.int32(0), jnp.int32(0)
    for doc in range(NDOC):
        end = end + scalars[BLOCKS + doc]
        start = jnp.where(own * BLOCK >= end, end, start)
    return own, start // BLOCK


def slot_of(slots, first, step):
    return slots[jnp.minimum(first + step, BLOCKS - 1)]


def slot_rows(slots, first, step):
    return pl.ds(pl.multiple_of(slot_of(slots, first, step) * BLOCK, BLOCK), BLOCK)


def key_block(kv, slots, first, step):
    slot = slot_of(slots, first, step)
    rows = pl.ds(pl.multiple_of((slot % 2) * BLOCK, BLOCK), BLOCK)
    return kv[slot // 2, rows, :]


def value_block(kv, far_values, slots, first, step, half):
    slot = slot_of(slots, first, step)
    return jnp.where(slot % 2 == half, kv[slot // 2, ROWS:, :], far_values[slot // 2])


def write_bias(scalars, own, first, bias):
    lane = lax.broadcasted_iota(jnp.int32, (1, HEAD_SIZE), 1)
    high = own * BLOCK + lane % BLOCK
    low, end = jnp.zeros_like(high), jnp.int32(0)
    for doc in range(NDOC):
        end = end + scalars[BLOCKS + doc]
        low = jnp.where(high >= end, end, low)
    for start, size in chunks():
        row = lax.broadcasted_iota(jnp.int32, (size, HEAD_SIZE), 0)
        position = first * BLOCK + start + row
        allowed = (position <= high) & (position >= low)
        bias[start : start + size, :] = jnp.where(allowed, 0.0, MASKED)


def probs_kernel(
    scalars,
    query,
    cotangent,
    kv,
    probs,
    value_part,
    far_sent,
    slots,
    keys,
    bias,
    scores,
    parts,
    low_parts,
    queries_in,
    gradients_in,
    done,
):
    fetches = [
        pltpu.make_async_copy(query, queries_in, done.at[0]),
        pltpu.make_async_copy(cotangent, gradients_in, done.at[1]),
    ]
    far = pltpu.make_async_copy(kv.at[:, pl.ds(ROWS, BLOCK), :], far_sent, done.at[6])
    for copy in fetches + [far]:
        copy.start()
    invert_order(scalars, slots)
    parts[...] = jnp.zeros_like(parts)
    firsts = []
    for half in range(2):
        own, first = span_of(scalars, half)
        firsts.append(first)
        for step in range(SPAN_BLOCKS):
            rows = slice(step * BLOCK, (step + 1) * BLOCK)
            keys[half, rows, :] = key_block(kv, slots, first, step)
        write_bias(scalars, own, first, bias.at[half])
    fetches[0].wait()
    tiles = 2 * GROUPS
    queries = [heads_of(queries_in, tile // GROUPS, tile % GROUPS) for tile in range(tiles)]
    tops = [jnp.full((8, LANES), MASKED, jnp.float32) for _ in range(tiles)]
    totals = [jnp.zeros((8, LANES), jnp.float32) for _ in range(tiles)]
    scaled = [None] * tiles

    def score(tile, start, size):
        rows = slice(start, start + size)
        half = tile // GROUPS
        raw = lax.dot_general(
            keys[half, rows, :], queries[tile], NT, preferred_element_type=jnp.float32
        )
        add = bias[half, rows, :]
        masked = raw * SCALE_LOG2 + jnp.concatenate([add, add], axis=1)
        scores[tile % 2, rows, :] = masked
        tops[tile] = jnp.maximum(tops[tile], fold_rows(masked, jnp.max))

    def weigh(tile, start, size):
        rows = slice(start, start + size)
        part = jnp.exp2(scores[tile % 2, rows, :] - tops[tile])
        probs[tile, rows, :] = part.astype(jnp.bfloat16)
        totals[tile] = totals[tile] + fold_rows(part, jnp.sum)

    def finish(tile):
        share = 1.0 / jnp.sum(totals[tile], axis=0, keepdims=True)
        by_row = jnp.broadcast_to(share, (HEAD_SIZE, LANES)).T
        full = heads_of(gradients_in, tile // GROUPS, tile % GROUPS).astype(jnp.float32)
        scaled[tile] = (full * by_row).astype(jnp.bfloat16)
        share = jnp.broadcast_to(share, (8, LANES))
        coarse = share.astype(jnp.bfloat16)
        rest = (share - coarse.astype(jnp.float32)).astype(jnp.bfloat16)
        probs[tile, SPAN:, :] = jnp.concatenate([coarse, rest], axis=0)

    def collect(half, start, size):
        rows = slice(start, start + size)
        add = sum(
            jnp.dot(probs[tile, rows, :], scaled[tile], preferred_element_type=jnp.float32)
            for tile in range(half * GROUPS, (half + 1) * GROUPS)
        )
        for step in range(size // BLOCK):
            target = slot_rows(slots, firsts[half], start // BLOCK + step)
            parts[target, :] += add[step * BLOCK : (step + 1) * BLOCK]

    for start, size in chunks():
        score(0, start, size)
    fetches[1].wait()
    for tile in range(tiles):
        tops[tile] = jnp.max(tops[tile], axis=0, keepdims=True)
        for start, size in chunks():
            if tile + 1 < tiles:
                score(tile + 1, start, size)
            weigh(tile, start, size)
            if tile == tiles - 1:
                collect(0, start, size)
        finish(tile)
    for start, size in chunks():
        collect(1, start, size)
    copies = []
    for piece in range(4):
        rows = pl.ds(piece * KEYS // 4, KEYS // 4)
        low_parts[rows, :] = parts[rows, :].astype(jnp.bfloat16)
        copies.append(
            pltpu.make_async_copy(
                low_parts.at[rows, :], value_part.at[rows, :], done.at[2 + piece]
            )
        )
        copies[-1].start()
    for copy in copies + [far]:
        copy.wait()


def grads_kernel(
    scalars,
    query,
    output,
    cotangent,
    kv,
    far_values,
    probs,
    zero,
    one,
    two,
    three,
    key_sent,
    key_kept,
    stacked,
    dscores_out,
    keys_out,
    slots,
    values,
    parts,
    queries_in,
    output_in,
    gradients_in,
    staged,
    kept,
    done,
):
    fetches = [
        pltpu.make_async_copy(source, target, done.at[index])
        for index, (source, target) in enumerate(
            ((cotangent, gradients_in), (output, output_in), (query, queries_in))
        )
    ]
    stacks = [
        pltpu.make_async_copy(piece.at[1], staged.at[relative], done.at[3 + relative])
        for relative, piece in enumerate((zero, one, two, three))
    ]
    stores = [
        pltpu.make_async_copy(staged.at[relative], stacked.at[relative], done.at[3 + relative])
        for relative in range(4)
    ]
    for copy in fetches + stacks:
        copy.start()
    me = scalars[BLOCKS + NDOC]
    invert_order(scalars, slots)
    parts[...] = jnp.zeros_like(parts)
    firsts = []
    for half in range(2):
        _, first = span_of(scalars, half)
        firsts.append(first)
        for step in range(SPAN_BLOCKS):
            rows = slice(step * BLOCK, (step + 1) * BLOCK)
            keys_out[half, rows, :] = key_block(kv, slots, first, step)
            values[half, rows, :] = value_block(kv, far_values, slots, first, step, me // 8)
    for copy in fetches:
        copy.wait()
    for half in range(2):
        first = firsts[half]
        queries, gradients, deltas, shares = [], [], [], []
        for group in range(GROUPS):
            queries.append(heads_of(queries_in, half, group))
            gradients.append(heads_of(gradients_in, half, group))
            forward = heads_of(output_in, half, group).astype(jnp.float32)
            product = gradients[group].astype(jnp.float32) * forward
            deltas.append(jnp.sum(product.T, axis=0, keepdims=True))
            pieces = probs[half * GROUPS + group, SPAN:, :].astype(jnp.float32)
            shares.append(pieces[:1] + pieces[8:9])
        for start, size in chunks(WIDE_CHUNK):
            rows = slice(start, start + size)
            add = 0.0
            for group in range(GROUPS):
                dprobs = lax.dot_general(
                    values[half, rows, :],
                    gradients[group],
                    NT,
                    preferred_element_type=jnp.float32,
                )
                weight = probs[half * GROUPS + group, rows, :].astype(jnp.float32) * shares[group]
                dscores = (weight * (dprobs - deltas[group])).astype(jnp.bfloat16)
                add = add + jnp.dot(dscores, queries[group], preferred_element_type=jnp.float32)
                dscores_out[half * GROUPS + group, rows, :] = dscores
            for step in range(size // BLOCK):
                target = slot_rows(slots, first, start // BLOCK + step)
                parts[target, :] += add[step * BLOCK : (step + 1) * BLOCK]
        if half == 0:
            for copy, store in zip(stacks, stores):
                copy.wait()
                store.start()
    keep = pltpu.make_async_copy(kept, key_kept, done.at[7])
    for half, part in enumerate((kept, key_sent)):
        for slot, relative in enumerate((0, 7, 2, 5, 1, 6, 3, 4)):
            start = pl.multiple_of((me ^ (half * 8 + relative)) * ROWS, ROWS)
            part[slot] = (parts[pl.ds(start, ROWS), :] * SCALE).astype(part.dtype)
        if half == 0:
            keep.start()
    for copy in stores + [keep]:
        copy.wait()


def query_kernel(keys, dscores, query_grad, key_turned, staged, done):
    for half in range(2):
        key_turned[...] = keys[half].T
        for group in range(GROUPS):
            turned = jnp.dot(
                key_turned[...], dscores[half * GROUPS + group], preferred_element_type=jnp.float32
            )
            by_row = (turned * SCALE).T.astype(jnp.bfloat16)
            for head in range(GROUP):
                column = (group * GROUP + head) * HEAD_SIZE
                staged[
                    half * BLOCK : (half + 1) * BLOCK, column : column + HEAD_SIZE
                ] = by_row[head * BLOCK : (head + 1) * BLOCK]
    copy = pltpu.make_async_copy(staged, query_grad, done)
    copy.start()
    copy.wait()


def query_product(keys, dscores):
    return pl.pallas_call(
        query_kernel,
        in_specs=[VMEM_SPEC] * 2,
        out_specs=HBM_SPEC,
        out_shape=pltpu.HBM((ROWS, QUERY_HEADS * HEAD_SIZE), jnp.bfloat16),
        scratch_shapes=[
            pltpu.VMEM((HEAD_SIZE, SPAN), jnp.bfloat16),
            pltpu.VMEM((ROWS, QUERY_HEADS * HEAD_SIZE), jnp.bfloat16),
            pltpu.SemaphoreType.DMA,
        ],
        compiler_params=PARAMS,
        name="query_product",
    )(keys, dscores)


def in_vmem(array):
    return pltpu.with_memory_space_constraint(array, pltpu.VMEM)


def in_hbm(array):
    return pltpu.with_memory_space_constraint(array, pltpu.HBM)


VMEM_SPEC = pl.BlockSpec(memory_space=pltpu.VMEM)
HBM_SPEC = pl.BlockSpec(memory_space=pltpu.HBM)
SMEM_SPEC = pl.BlockSpec(memory_space=pltpu.SMEM)
PARAMS = pltpu.CompilerParams(vmem_limit_bytes=VMEM_LIMIT)


def attention_probs(scalars, query, cotangent, kv):
    return pl.pallas_call(
        probs_kernel,
        in_specs=[SMEM_SPEC, HBM_SPEC, HBM_SPEC, VMEM_SPEC],
        out_specs=[VMEM_SPEC, HBM_SPEC, HBM_SPEC],
        out_shape=[
            jax.ShapeDtypeStruct((2 * GROUPS, SPAN + 16, LANES), jnp.bfloat16),
            pltpu.HBM((KEYS, HEAD_SIZE), jnp.bfloat16),
            pltpu.HBM((N_CTX, BLOCK, HEAD_SIZE), jnp.bfloat16),
        ],
        scratch_shapes=[
            pltpu.SMEM((BLOCKS,), jnp.int32),
            pltpu.VMEM((2, SPAN, HEAD_SIZE), jnp.bfloat16),
            pltpu.VMEM((2, SPAN, HEAD_SIZE), jnp.float32),
            pltpu.VMEM((2, SPAN, LANES), jnp.float32),
            pltpu.VMEM((KEYS, HEAD_SIZE), jnp.float32),
            pltpu.VMEM((KEYS, HEAD_SIZE), jnp.bfloat16),
            pltpu.VMEM((ROWS, QUERY_HEADS * HEAD_SIZE), jnp.bfloat16),
            pltpu.VMEM((ROWS, QUERY_HEADS * HEAD_SIZE), jnp.bfloat16),
            pltpu.SemaphoreType.DMA((7,)),
        ],
        compiler_params=PARAMS,
        name="probs_and_value_part",
    )(scalars, in_hbm(query), in_hbm(cotangent), kv)


def attention_grads(scalars, query, output, cotangent, kv, far_values, probs, pieces):
    return pl.pallas_call(
        grads_kernel,
        in_specs=[SMEM_SPEC] + [HBM_SPEC] * 3 + [VMEM_SPEC] * 3 + [HBM_SPEC] * 4,
        out_specs=[VMEM_SPEC] + [HBM_SPEC] * 2 + [VMEM_SPEC] * 2,
        out_shape=[
            jax.ShapeDtypeStruct((8, ROWS, HEAD_SIZE), jnp.bfloat16),
            pltpu.HBM((8, ROWS, HEAD_SIZE), jnp.bfloat16),
            pltpu.HBM((4,) + pieces[0].shape[1:], jnp.bfloat16),
            jax.ShapeDtypeStruct((2 * GROUPS, SPAN, LANES), jnp.bfloat16),
            jax.ShapeDtypeStruct((2, SPAN, HEAD_SIZE), jnp.bfloat16),
        ],
        scratch_shapes=[
            pltpu.SMEM((BLOCKS,), jnp.int32),
            pltpu.VMEM((2, SPAN, HEAD_SIZE), jnp.bfloat16),
            pltpu.VMEM((KEYS, HEAD_SIZE), jnp.float32),
            pltpu.VMEM((ROWS, QUERY_HEADS * HEAD_SIZE), jnp.bfloat16),
            pltpu.VMEM((ROWS, QUERY_HEADS * HEAD_SIZE), jnp.bfloat16),
            pltpu.VMEM((ROWS, QUERY_HEADS * HEAD_SIZE), jnp.bfloat16),
            pltpu.VMEM((4,) + pieces[0].shape[1:], jnp.bfloat16),
            pltpu.VMEM((8, ROWS, HEAD_SIZE), jnp.bfloat16),
            pltpu.SemaphoreType.DMA((8,)),
        ],
        compiler_params=PARAMS,
        name="key_part",
    )(scalars, *map(in_hbm, (query, output, cotangent)), kv, far_values, probs, *map(in_hbm, pieces))


def load_kernel(zero, one, two, three, partner, sources, done):
    copies = []
    for relative, mine in enumerate((zero, one, two, three)):
        for other, source in enumerate((mine.at[0], partner.at[relative])):
            target = sources.at[relative, pl.ds(other * ROWS, ROWS), :]
            copies.append(pltpu.make_async_copy(source, target, done.at[2 * relative + other]))
    for copy in copies:
        copy.start()
    for copy in copies:
        copy.wait()


def load_inputs(pieces, partner):
    return pl.pallas_call(
        load_kernel,
        in_specs=[HBM_SPEC] * 5,
        out_specs=VMEM_SPEC,
        out_shape=pltpu.VMEM((4, 2 * ROWS, pieces[0].shape[2]), jnp.bfloat16),
        scratch_shapes=[pltpu.SemaphoreType.DMA((8,))],
        compiler_params=PARAMS,
        name="load_inputs",
    )(*map(in_hbm, pieces), in_hbm(partner))


def split_kernel(place, inputs, zero, one, two, three, staged, done):
    x, core = place[0], place[1]
    fetches, stores = [], []
    for relative, part in enumerate((zero, one, two, three)):
        for other in range(2):
            index = 2 * relative + other
            near = (x ^ relative) * 2 + (core ^ other)
            for low in range(2):
                start = pl.multiple_of((low * 8 + near) * WIDTH, WIDTH)
                fetches.append(
                    pltpu.make_async_copy(
                        inputs.at[:, pl.ds(start, WIDTH)],
                        staged.at[index, :, pl.ds(low * WIDTH, WIDTH)],
                        done.at[2 * index + low],
                    )
                )
            stores.append(
                pltpu.make_async_copy(staged.at[index], part.at[other], done.at[2 * index])
            )
    for copy in fetches:
        copy.start()
    for index, store in enumerate(stores):
        fetches[2 * index].wait()
        fetches[2 * index + 1].wait()
        store.start()
    for store in stores:
        store.wait()


def split_inputs(place, inputs):
    return pl.pallas_call(
        split_kernel,
        in_specs=[SMEM_SPEC, HBM_SPEC],
        out_specs=[HBM_SPEC] * 4,
        out_shape=[pltpu.HBM((2, ROWS, 2 * WIDTH), jnp.bfloat16)] * 4,
        scratch_shapes=[
            pltpu.VMEM((8, ROWS, 2 * WIDTH), jnp.bfloat16),
            pltpu.SemaphoreType.DMA((16,)),
        ],
        compiler_params=PARAMS,
        name="split_inputs",
    )(place, in_hbm(inputs))


def fold(kept, received, next_kept, next_sent):
    total = kept[...].astype(jnp.float32) + received[...].astype(jnp.float32)
    count = next_kept.shape[0]
    next_kept[...] = total[:count]
    next_sent[...] = total[count:].astype(jnp.bfloat16)


def halves_of(kept):
    half = (kept.shape[0] // 2,) + kept.shape[1:]
    return [
        jax.ShapeDtypeStruct(half, jnp.float32),
        jax.ShapeDtypeStruct(half, jnp.bfloat16),
    ]


def spread_kernel(
    blocks, kept, received, after, value_grad, spread, next_kept, next_sent, arrived, low, old, done
):
    count = blocks.shape[0]
    fetches = [
        pltpu.make_async_copy(blocks.at[block], arrived.at[block], done.at[block])
        for block in range(count)
    ]
    fetch_old = pltpu.make_async_copy(kept, old, done.at[count])
    for copy in fetches + [fetch_old]:
        copy.start()
    total = 0.0
    for block in range(count):
        fetches[block].wait()
        total = total + arrived[block].astype(jnp.float32)
    total = total.astype(jnp.bfloat16)
    low[...] = total
    value_grad[...] = total
    stores = [
        pltpu.make_async_copy(low, spread.at[copy], done.at[copy])
        for copy in range(spread.shape[0])
    ]
    for copy in stores:
        copy.start()
    fetch_old.wait()
    fold(old, received, next_kept, next_sent)
    for copy in stores:
        copy.wait()


def sum_and_spread(blocks, count, kept, received, after):
    shape = blocks.shape[1:]
    return pl.pallas_call(
        spread_kernel,
        in_specs=[HBM_SPEC, HBM_SPEC, VMEM_SPEC, HBM_SPEC],
        out_specs=[VMEM_SPEC, HBM_SPEC, VMEM_SPEC, VMEM_SPEC],
        out_shape=[
            jax.ShapeDtypeStruct(shape, jnp.bfloat16),
            pltpu.HBM((count,) + shape, jnp.bfloat16),
        ]
        + halves_of(kept),
        scratch_shapes=[
            pltpu.VMEM(blocks.shape, jnp.bfloat16),
            pltpu.VMEM(shape, jnp.bfloat16),
            pltpu.VMEM(kept.shape, jnp.bfloat16),
            pltpu.SemaphoreType.DMA((blocks.shape[0] + 1,)),
        ],
        compiler_params=PARAMS,
        name="sum_and_spread",
    )(in_hbm(blocks), in_hbm(kept), received, in_hbm(after))


def join_kernel(key, value, joined, both, done):
    copies = []
    for half in range(2):
        both[half, :ROWS] = key[...]
        both[half, ROWS:] = value[half * BLOCK : (half + 1) * BLOCK]
        for copy in range(half * N_CTX // 2, (half + 1) * N_CTX // 2):
            copies.append(pltpu.make_async_copy(both.at[half], joined.at[copy], done.at[copy]))
            copies[-1].start()
    for copy in copies:
        copy.wait()


def join_keys_values(key, value):
    return pl.pallas_call(
        join_kernel,
        in_specs=[VMEM_SPEC] * 2,
        out_specs=HBM_SPEC,
        out_shape=pltpu.HBM((N_CTX, ROWS + BLOCK, HEAD_SIZE), jnp.bfloat16),
        scratch_shapes=[
            pltpu.VMEM((2, ROWS + BLOCK, HEAD_SIZE), jnp.bfloat16),
            pltpu.SemaphoreType.DMA((N_CTX,)),
        ],
        name="join_keys_values",
    )(key, value)


def weight_kernel(place, values, sources, kept, received, weight_part, next_kept, next_sent):
    x, core = place[0], place[1]
    total = 0.0
    for relative in range(4):
        near = (x ^ relative) * 2
        lhs = jnp.concatenate([values[near + core].T, values[near + (1 - core)].T], axis=1)
        total = total + jnp.dot(lhs, sources[relative], preferred_element_type=jnp.float32)
    for block in range(weight_part.shape[0] // HEAD_SIZE):
        columns = pl.ds(block * HEAD_SIZE, HEAD_SIZE)
        weight_part[columns, :] = total[:, block * HEAD_SIZE : (block + 1) * HEAD_SIZE].T.astype(
            jnp.bfloat16
        )
    fold(kept, received, next_kept, next_sent)


def weight_product(place, values, sources, kept, received):
    return pl.pallas_call(
        weight_kernel,
        in_specs=[SMEM_SPEC] + [VMEM_SPEC] * 4,
        out_specs=[VMEM_SPEC] * 3,
        out_shape=[jax.ShapeDtypeStruct((2 * WIDTH, HEAD_SIZE), jnp.bfloat16)] + halves_of(kept),
        compiler_params=PARAMS,
        name="weight_product",
    )(place, values, in_vmem(sources), kept, received)


def last_sums_kernel(blocks, kept, received, weight_grad, key_grad):
    total = blocks[0].astype(jnp.float32)
    for block in range(1, blocks.shape[0]):
        total = total + blocks[block].astype(jnp.float32)
    weight_grad[...] = total
    key_grad[...] = (kept[:1] + received[...].astype(jnp.float32)).astype(jnp.bfloat16)


def last_sums(blocks, kept, received):
    return pl.pallas_call(
        last_sums_kernel,
        in_specs=[VMEM_SPEC] * 3,
        out_specs=[VMEM_SPEC] * 2,
        out_shape=[
            jax.ShapeDtypeStruct(blocks.shape[1:], jnp.float32),
            jax.ShapeDtypeStruct(received.shape, jnp.bfloat16),
        ],
        compiler_params=PARAMS,
        name="last_sums",
    )(blocks, kept, received)


def exchange(blocks, axes):
    return lax.all_to_all(blocks, axes, 0, 0, tiled=False)


def swapped(block, axis, shift):
    count = lax.axis_size(axis)
    return lax.ppermute(block, axis, [(i, i ^ shift) for i in range(count)])


def local(query, key, value, output, output_cotangent, inputs, doc_lengths, block_order):
    scalars = jnp.concatenate(
        [block_order, doc_lengths[0], lax.axis_index(CTX).astype(jnp.int32)[None]]
    )
    place = jnp.stack([lax.axis_index("x"), lax.axis_index("core")]).astype(jnp.int32)
    near_count, far_count = lax.axis_size(NEAR), lax.axis_size(FAR)
    kv = exchange(join_keys_values(key[0], value[0]), CTX)

    parts = split_inputs(place, inputs)
    pieces = [parts[0]] + [swapped(parts[r], "x", r) for r in range(1, 4)]
    probs, value_part, far_sent = attention_probs(scalars, query[0], output_cotangent[0], kv)
    far_values = swapped(far_sent, "yhi", 1)
    value_blocks = exchange(value_part.reshape(N_CTX, ROWS, HEAD_SIZE), CTX)
    key_sent, key_kept, stacked, dscores, reached = attention_grads(
        scalars, query[0], output[0], output_cotangent[0], kv, far_values, probs, pieces
    )
    query_grad = query_product(reached, dscores)
    partner = swapped(stacked, "core", 1)
    sources = load_inputs(pieces, partner)
    value_grad, spread, key_kept, key_sent = sum_and_spread(
        value_blocks, near_count, key_kept, swapped(key_sent, "yhi", 1), query_grad
    )
    near_values = exchange(spread, NEAR)
    weight_part, key_kept, key_sent = weight_product(
        place, near_values, sources, key_kept, swapped(key_sent, "z", 1)
    )
    weight_blocks = exchange(weight_part.reshape(far_count, -1, HEAD_SIZE), FAR)
    key_sum = key_kept + swapped(key_sent, "z", 2).astype(jnp.float32)
    received = swapped(key_sum[1:].astype(jnp.bfloat16), "z", 7)
    weight_grad, key_grad = last_sums(weight_blocks, key_sum, received)
    return query_grad[None], key_grad, value_grad[None], weight_grad


def solution(mesh):
    fine = Mesh(
        mesh.devices.reshape(2, 4, 2, 2, 8), ("ylo", "x", "core", "yhi", "z")
    )
    dp = ("ylo", "x", "core")
    tokens = P(dp, CTX, None)
    flat = P(dp + CTX, None)
    return jax.shard_map(
        local,
        mesh=fine,
        in_specs=(tokens,) * 5 + (flat, P(dp, None), P()),
        out_specs=(tokens, tokens, tokens, flat),
        check_vma=False,
    )
```
